32 devices in a mesh: row: 8 (over y, x, core), col: 4 (over z).
Axes of the slice: x: 2, y: 2, z: 4, core: 2. Of those that a mesh axis runs over, the one named last changes fastest.
Arguments:
- tokens: bfloat16 [1536, 18432], P('col', 'row'), may hold values from -6 to 6
- out_grad: bfloat16 [1536, 18432], P('col', 'row'), may hold values from -6 to 6
- logratio: float32 [1536], P('col'), as said below
- token_session: int32 [1536], P('col'), may hold values from 0 to 7
- token_position: int32 [1536], P('col'), may hold values from 0 to 3
- pad_mask: int32 [1536], P('col'), may hold values from 0 to 1, as said below
- w_in: float32 [18432, 3072], P('row', 'col'), may hold values from -0.046875 to 0.046875
- m_in: float32 [18432, 3072], P('row', 'col'), may hold values from -6 to 6
- v_in: float32 [18432, 3072], P('row', 'col'), may hold values from 0.2 to 5
- w_out: float32 [3072, 18432], P('col', 'row'), may hold values from -0.109375 to 0.109375
- m_out: float32 [3072, 18432], P('col', 'row'), may hold values from -6 to 6
- v_out: float32 [3072, 18432], P('col', 'row'), may hold values from 0.2 to 5
Outputs:
- new_w_in: float32 [18432, 3072], P('row', 'col')
- new_m_in: float32 [18432, 3072], P('row', 'col')
- new_v_in: float32 [18432, 3072], P('row', 'col')
- new_w_out: float32 [3072, 18432], P('col', 'row')
- new_m_out: float32 [3072, 18432], P('col', 'row')
- new_v_out: float32 [3072, 18432], P('col', 'row')
The draws below stay inside these ranges and needn't reach their ends.
Inputs may be any that keep to these rules, and one draw needn't show every extreme that they name: `pad_mask`: some tokens are padding in every draw. `logratio`: Real-valued log-probability differences of order one.
All inputs are finite; a program needn't handle non-finite values.
Results may differ from the reference program's by a relative error of at most 0.0013.
Values may be sent and summed in bfloat16 or wider, within the bound.
No kernel may reach another device: no remote copies, remote signals or barrier semaphores. Data moves between devices by JAX's collectives and lax.ppermute only.
A program may use at most 256 MiB of HBM per device.

```python
import math
import jax
import jax.numpy as jnp
from jax import lax

D = 18432
F = 3072
SESSIONS = 8
LIST = 4
TOKENS = 1536


def draw_logratio(key, part):
    key = jax.random.fold_in(key, 7)
    place = jnp.arange(TOKENS, dtype=jnp.float32) / TOKENS
    scale = 0.5 + place
    values = jax.random.normal(key, (TOKENS,), jnp.float32) * scale
    return values.astype(jnp.float32)


def draw_pad_mask(key, part):
    key = jax.random.fold_in(key, 11)
    first_key, second_key = jax.random.split(key)
    levels = jax.random.randint(first_key, (TOKENS,), 0, 4)
    forced = jax.random.randint(second_key, (), 0, TOKENS)
    places = jnp.arange(TOKENS, dtype=jnp.int32)
    keep = (levels != 0) & (places != forced)
    return jnp.where(keep, 1, 0).astype(jnp.int32)


def plant(result, key, low, largest):
    longest = result.shape.index(max(result.shape))
    spots = []
    for shift in (0, 1):
        where = [jax.random.randint(jax.random.fold_in(key, axis), (), 0, length) for axis, length in enumerate(result.shape)]
        where[longest] = (where[longest] + shift) % result.shape[longest]
        spots.append(tuple(where))
    return result.at[spots[0]].set(low).at[spots[1]].set(largest)


def block_levels(own_key, dims, cuts, low, largest):
    def one(dim, shards_of):
        draws = jax.random.uniform(jax.random.fold_in(jax.random.fold_in(own_key, 6), dim), (shards_of,), jnp.float32, low / len(cuts), largest / len(cuts))
        return jnp.repeat(jnp.exp(draws), dims[dim] // shards_of).reshape((-1,) + (1,) * (len(dims) - dim - 1))

    factor_of = one(*cuts[0])
    for cut in cuts[1:]:
        factor_of = factor_of * one(*cut)
    return factor_of


def normal_values(key, dims, spread, most, shards=(), kind=jnp.bfloat16):
    values = spread * jax.random.normal(key, dims, jnp.float32)
    if shards:
        values = values * block_levels(key, dims, shards, -0.22, 0.18)
    return jnp.clip(values, -most, most).astype(kind)


def setup_inputs(seed: int = 0) -> dict:
    key_list = jax.random.split(jax.random.key(seed), 13)
    tokens = normal_values(key_list[0], (TOKENS, D), 1.0, 6.0, ((0, 4), (1, 8)))
    out_grad = normal_values(key_list[1], (TOKENS, D), 1.0, 6.0, ((0, 4), (1, 8)))
    logratio = draw_logratio(jax.random.fold_in(key_list[12], 71), 0)
    token_session = plant(jax.random.randint(key_list[3], (TOKENS,), 0, SESSIONS), jax.random.fold_in(key_list[3], 1), 0, SESSIONS - 1).astype(jnp.int32)
    token_position = plant(jax.random.randint(key_list[4], (TOKENS,), 0, LIST), jax.random.fold_in(key_list[4], 1), 0, LIST - 1).astype(jnp.int32)
    pad_mask = draw_pad_mask(jax.random.fold_in(key_list[12], 71), 0)
    w_in = normal_values(key_list[6], (D, F), D ** -0.5, 0.046875, ((0, 8), (1, 4)), jnp.float32)
    m_in = normal_values(key_list[7], (D, F), 1.0, 6.0, ((0, 8), (1, 4)), jnp.float32)
    v_in = jnp.clip(jnp.exp(math.log(5.0) - 3.218876 * jax.random.uniform(key_list[8], (D, F), jnp.float32) ** block_levels(key_list[8], (D, F), ((0, 8), (1, 4)), -0.2, 0.2)), 0.2, 5.0)
    w_out = normal_values(key_list[9], (F, D), F ** -0.5, 0.109375, ((0, 4), (1, 8)), jnp.float32)
    m_out = normal_values(key_list[10], (F, D), 1.0, 6.0, ((0, 4), (1, 8)), jnp.float32)
    v_out = jnp.clip(jnp.exp(math.log(5.0) - 3.218876 * jax.random.uniform(key_list[11], (F, D), jnp.float32) ** block_levels(key_list[11], (F, D), ((0, 4), (1, 8)), -0.2, 0.2)), 0.2, 5.0)
    return {"tokens": tokens, "out_grad": out_grad, "logratio": logratio, "token_session": token_session, "token_position": token_position, "pad_mask": pad_mask, "w_in": w_in, "m_in": m_in, "v_in": v_in, "w_out": w_out, "m_out": m_out, "v_out": v_out}


def listwise_grad(scores):
    s = scores.reshape(SESSIONS, LIST)
    later = s[:, None, :] - s[:, :, None]
    order = jnp.arange(LIST)
    after = (order[None, :] > order[:, None]).astype(jnp.float32)
    before = (order[None, :] < order[:, None]).astype(jnp.float32)
    worse = -lax.optimization_barrier(jnp.sum(after[None] * jax.nn.sigmoid(later), axis=2))
    better = lax.optimization_barrier(jnp.sum(before[None] * jax.nn.sigmoid(-later), axis=2))
    return (worse + better).reshape(SESSIONS * LIST)

def adamw(weight, first, second, grad):
    new_first = 0.9 * first + 0.1 * grad
    new_second = 0.95 * second + 0.05 * grad * grad
    step = new_first / (1.0 - 0.9 ** 20) / (jnp.sqrt(new_second / (1.0 - 0.95 ** 20)) + 1e-08) + 0.1 * weight
    return (weight - 0.0003 * step, new_first, new_second)

def reference(tokens, out_grad, logratio, token_session, token_position, pad_mask, w_in, m_in, v_in, w_out, m_out, v_out):
    response = token_session * LIST + token_position
    onehot = (response[:, None] == jnp.arange(SESSIONS * LIST, dtype=jnp.int32)[None, :]).astype(jnp.float32)
    live = pad_mask.astype(jnp.float32)
    factor = math.sqrt(SESSIONS * LIST / TOKENS)
    scores = factor * lax.optimization_barrier(jnp.sum(onehot * (live * logratio)[:, None], axis=0))
    response_grad = listwise_grad(scores)
    coeff = 0.1 * live * lax.optimization_barrier(jnp.sum(onehot * response_grad[None, :], axis=1))
    dy = (coeff[:, None] * out_grad.astype(jnp.float32)).astype(jnp.bfloat16)
    w_in16 = w_in.astype(jnp.bfloat16)
    w_out16 = w_out.astype(jnp.bfloat16)
    pre = jnp.dot(tokens, w_in16, preferred_element_type=jnp.float32)
    back = jnp.dot(dy, w_out16.T, preferred_element_type=jnp.float32)
    positive = jnp.maximum(pre, 0.0)
    act = (positive * positive).astype(jnp.bfloat16)
    dpre = (back * 2.0 * positive).astype(jnp.bfloat16)
    grad_in = jnp.dot(tokens.T, dpre, preferred_element_type=jnp.float32)
    grad_out = jnp.dot(act.T, dy, preferred_element_type=jnp.float32)
    new_w_in, new_m_in, new_v_in = adamw(w_in, m_in, v_in, grad_in)
    new_w_out, new_m_out, new_v_out = adamw(w_out, m_out, v_out, grad_out)
    return (new_w_in, new_m_in, new_v_in, new_w_out, new_m_out, new_v_out)
```

```python
import functools
import math

import jax
import jax.numpy as jnp
from jax import lax
from jax.experimental import pallas as pl
from jax.experimental.pallas import tpu as pltpu
from jax.sharding import PartitionSpec as P

SESSIONS = 8
LIST = 4


def listwise_grad(scores):
    s = scores.reshape(SESSIONS, LIST)
    later = s[:, None, :] - s[:, :, None]
    order = jnp.arange(LIST)
    after = (order[None, :] > order[:, None]).astype(jnp.float32)
    before = (order[None, :] < order[:, None]).astype(jnp.float32)
    worse = -jnp.sum(after[None] * jax.nn.sigmoid(later), axis=2)
    better = jnp.sum(before[None] * jax.nn.sigmoid(-later), axis=2)
    return (worse + better).reshape(SESSIONS * LIST)


def adamw(weight, first, second, grad):
    new_first = 0.9 * first + 0.1 * grad
    new_second = 0.95 * second + 0.05 * grad * grad
    step = (
        new_first / (1.0 - 0.9**20) / (jnp.sqrt(new_second / (1.0 - 0.95**20)) + 1e-08)
        + 0.1 * weight
    )
    return (weight - 0.0003 * step, new_first, new_second)


def over_rows(left, right):
    return lax.dot_general(
        left, right, (((0,), (0,)), ((), ())), preferred_element_type=jnp.float32
    )


def against(left, right):
    return lax.dot_general(
        left, right, (((1,), (1,)), ((), ())), preferred_element_type=jnp.float32
    )


def block_of(size, most):
    block = most
    while size % block:
        block -= 128
    return block


def grad_kernel(parts, *refs):
    lefts, rights, out = refs[:parts], refs[parts : 2 * parts], refs[2 * parts]
    total = over_rows(lefts[0][...], rights[0][...])
    for left, right in zip(lefts[1:], rights[1:]):
        total += over_rows(left[...], right[...])
    out[...] = total


def grad_sum(lefts, rights, most):
    rows, height = lefts[0].shape
    width = rights[0].shape[1]
    parts = len(lefts)
    block = block_of(height, most)
    return pl.pallas_call(
        functools.partial(grad_kernel, parts),
        grid=(height // block,),
        in_specs=[pl.BlockSpec((rows, block), lambda i: (0, i))] * parts
        + [pl.BlockSpec((rows, width), lambda i: (0, 0))] * parts,
        out_specs=pl.BlockSpec((block, width), lambda i: (i, 0)),
        out_shape=jax.ShapeDtypeStruct((height, width), jnp.float32),
        compiler_params=pltpu.CompilerParams(vmem_limit_bytes=44 * 2**20),
        cost_estimate=pl.CostEstimate(
            flops=2 * parts * rows * height * width,
            bytes_accessed=4 * height * width + 2 * parts * rows * (height + width),
            transcendentals=0,
        ),
    )(*lefts, *rights)


def update_kernel(left, right, grad, w, m, v, new_w, new_m, new_v):
    total = grad[...] + over_rows(left[...], right[...])
    new_w[...], new_m[...], new_v[...] = adamw(w[...], m[...], v[...], total)


def update(left, right, grad, w, m, v, most):
    rows, height = left.shape
    width = right.shape[1]
    block = block_of(height, most)
    panel = pl.BlockSpec((block, width), lambda i: (i, 0))
    shape = jax.ShapeDtypeStruct((height, width), jnp.float32)
    return pl.pallas_call(
        update_kernel,
        grid=(height // block,),
        in_specs=[
            pl.BlockSpec((rows, block), lambda i: (0, i)),
            pl.BlockSpec((rows, width), lambda i: (0, 0)),
            panel,
            panel,
            panel,
            panel,
        ],
        out_specs=[panel] * 3,
        out_shape=[shape] * 3,
        compiler_params=pltpu.CompilerParams(vmem_limit_bytes=44 * 2**20),
        cost_estimate=pl.CostEstimate(
            flops=2 * rows * height * width,
            bytes_accessed=7 * 4 * height * width + 2 * rows * (height + width),
            transcendentals=2 * height * width,
        ),
    )(left, right, grad, w, m, v)


def link_pairs(n, first, step):
    pairs = []
    for low in range(first, n - 1, 2):
        if low - (step - 1) >= 0:
            pairs.append((low, low + 1))
        if low + step <= n - 1:
            pairs.append((low + 1, low))
    return pairs


def arrivals(n, c):
    order = []
    for step in range(1, n):
        from_right, from_left = c + step <= n - 1, c - step >= 0
        over = (from_right, from_left) if c % 2 == 0 else (from_left, from_right)
        order += [(links, step) for links in (0, 1) if over[links]]
    return order


def line_gather(shard, axis):
    n = lax.axis_size(axis)
    here = lax.axis_index(axis)
    came = {(0, 0): shard, (1, 0): shard}
    for step in range(1, n):
        for links in (0, 1):
            pairs = link_pairs(n, links, step)
            if pairs:
                came[links, step] = lax.ppermute(came[1 - links, step - 1], axis, pairs)
    slots = [shard]
    tables = [arrivals(n, c) for c in range(n)]
    for slot in range(n - 1):
        users = {}
        for c in range(n):
            users.setdefault(tables[c][slot], []).append(c)
        choice = None
        for source, places in users.items():
            if choice is None:
                choice = came[source]
            else:
                mine = functools.reduce(jnp.logical_or, [here == c for c in places])
                choice = jnp.where(mine, came[source], choice)
        slots.append(choice)
    return slots


def row_sum(parts, earlier):
    if earlier is not None:
        parts, _ = lax.optimization_barrier((parts, earlier))
    return lax.psum(parts, "row")


def on_device(
    tokens,
    out_grad,
    logratio,
    token_session,
    token_position,
    pad_mask,
    w_in,
    m_in,
    v_in,
    w_out,
    m_out,
    v_out,
):
    n = lax.axis_size("col")
    token_slots = line_gather(tokens, "col")
    all_rows = tokens.shape[0] * n
    response = token_session * LIST + token_position
    onehot = (response[:, None] == jnp.arange(SESSIONS * LIST, dtype=jnp.int32)[None, :]).astype(
        jnp.float32
    )
    live = pad_mask.astype(jnp.float32)
    local_sums = jnp.sum(onehot * (live * logratio)[:, None], axis=0)
    factor = math.sqrt(SESSIONS * LIST / all_rows)
    scores = factor * lax.psum(local_sums, "col")
    response_grad = listwise_grad(scores)
    coeff = 0.1 * live * jnp.sum(onehot * response_grad[None, :], axis=1)
    dy = (coeff[:, None] * out_grad.astype(jnp.float32)).astype(jnp.bfloat16)
    dy_slots = line_gather(dy, "col")
    w_in16, w_out16 = lax.optimization_barrier(
        (w_in.astype(jnp.bfloat16), w_out.astype(jnp.bfloat16))
    )
    acts, dpres = [], []
    last = None
    for slot in range(n - 1):
        pre_part = jnp.dot(token_slots[slot], w_in16, preferred_element_type=jnp.float32)
        back_part = against(dy_slots[slot], w_out16)
        pre, back = last = row_sum((pre_part, back_part), last)
        positive = jnp.maximum(pre, 0.0)
        acts.append((positive * positive).astype(jnp.bfloat16))
        dpres.append((back * 2.0 * positive).astype(jnp.bfloat16))
    grad_in = grad_sum(token_slots[:-1], dpres, 256)
    grad_out = grad_sum(acts, dy_slots[:-1], 128)
    tokens_last, dy_last = token_slots[-1], dy_slots[-1]
    pre_part = jnp.dot(tokens_last, w_in16, preferred_element_type=jnp.float32)
    (pre,) = last = row_sum((pre_part,), last)
    positive = jnp.maximum(pre, 0.0)
    act = (positive * positive).astype(jnp.bfloat16)
    dy_last, grad_in, grad_out = lax.optimization_barrier((dy_last, grad_in, grad_out))
    (back,) = row_sum((against(dy_last, w_out16),), last)
    outs_out = update(act, dy_last, grad_out, w_out, m_out, v_out, 128)
    back, outs_out = lax.optimization_barrier((back, outs_out))
    dpre = (back * 2.0 * positive).astype(jnp.bfloat16)
    outs_in = update(tokens_last, dpre, grad_in, w_in, m_in, v_in, 256)
    return (*outs_in, *outs_out)


def solution(mesh):
    in_specs = (
        P("col", "row"),
        P("col", "row"),
        P("col"),
        P("col"),
        P("col"),
        P("col"),
        P("row", "col"),
        P("row", "col"),
        P("row", "col"),
        P("col", "row"),
        P("col", "row"),
        P("col", "row"),
    )
    out_specs = (
        P("row", "col"),
        P("row", "col"),
        P("row", "col"),
        P("col", "row"),
        P("col", "row"),
        P("col", "row"),
    )
    return jax.shard_map(
        on_device, mesh=mesh, in_specs=in_specs, out_specs=out_specs, check_vma=False
    )
```

```python
import functools
import math

import jax
import jax.numpy as jnp
from jax import lax
from jax.experimental import pallas as pl
from jax.experimental.pallas import tpu as pltpu
from jax.sharding import PartitionSpec as P

SESSIONS = 8
LIST = 4


def listwise_grad(scores):
    s = scores.reshape(SESSIONS, LIST)
    later = s[:, None, :] - s[:, :, None]
    order = jnp.arange(LIST)
    after = (order[None, :] > order[:, None]).astype(jnp.float32)
    before = (order[None, :] < order[:, None]).astype(jnp.float32)
    worse = -jnp.sum(after[None] * jax.nn.sigmoid(later), axis=2)
    better = jnp.sum(before[None] * jax.nn.sigmoid(-later), axis=2)
    return (worse + better).reshape(SESSIONS * LIST)


def adamw(weight, first, second, grad):
    new_first = 0.9 * first + 0.1 * grad
    new_second = 0.95 * second + 0.05 * grad * grad
    step = (
        new_first / (1.0 - 0.9**20) / (jnp.sqrt(new_second / (1.0 - 0.95**20)) + 1e-08)
        + 0.1 * weight
    )
    return (weight - 0.0003 * step, new_first, new_second)


def over_rows(left, right):
    return lax.dot_general(
        left, right, (((0,), (0,)), ((), ())), preferred_element_type=jnp.float32
    )


def against(left, right):
    return lax.dot_general(
        left, right, (((1,), (1,)), ((), ())), preferred_element_type=jnp.float32
    )


def block_of(size, most):
    block = most
    while size % block:
        block -= 128
    return block


def grad_kernel(parts, *refs):
    lefts, rights, out = refs[:parts], refs[parts : 2 * parts], refs[2 * parts]
    total = over_rows(lefts[0][...], rights[0][...])
    for left, right in zip(lefts[1:], rights[1:]):
        total += over_rows(left[...], right[...])
    out[...] = total


def grad_sum(lefts, rights, most):
    rows, height = lefts[0].shape
    width = rights[0].shape[1]
    parts = len(lefts)
    block = block_of(height, most)
    return pl.pallas_call(
        functools.partial(grad_kernel, parts),
        grid=(height // block,),
        in_specs=[pl.BlockSpec((rows, block), lambda i: (0, i))] * parts
        + [pl.BlockSpec((rows, width), lambda i: (0, 0))] * parts,
        out_specs=pl.BlockSpec((block, width), lambda i: (i, 0)),
        out_shape=jax.ShapeDtypeStruct((height, width), jnp.float32),
        compiler_params=pltpu.CompilerParams(vmem_limit_bytes=44 * 2**20),
        cost_estimate=pl.CostEstimate(
            flops=2 * parts * rows * height * width,
            bytes_accessed=4 * height * width + 2 * parts * rows * (height + width),
            transcendentals=0,
        ),
    )(*lefts, *rights)


def update_kernel(left, right, grad, w, m, v, new_w, new_m, new_v):
    total = grad[...] + over_rows(left[...], right[...])
    new_w[...], new_m[...], new_v[...] = adamw(w[...], m[...], v[...], total)


def update(left, right, grad, w, m, v, most):
    rows, height = left.shape
    width = right.shape[1]
    block = block_of(height, most)
    panel = pl.BlockSpec((block, width), lambda i: (i, 0))
    shape = jax.ShapeDtypeStruct((height, width), jnp.float32)
    return pl.pallas_call(
        update_kernel,
        grid=(height // block,),
        in_specs=[
            pl.BlockSpec((rows, block), lambda i: (0, i)),
            pl.BlockSpec((rows, width), lambda i: (0, 0)),
            panel,
            panel,
            panel,
            panel,
        ],
        out_specs=[panel] * 3,
        out_shape=[shape] * 3,
        compiler_params=pltpu.CompilerParams(vmem_limit_bytes=44 * 2**20),
        cost_estimate=pl.CostEstimate(
            flops=2 * rows * height * width,
            bytes_accessed=7 * 4 * height * width + 2 * rows * (height + width),
            transcendentals=2 * height * width,
        ),
    )(left, right, grad, w, m, v)


def link_pairs(n, first, step):
    pairs = []
    for low in range(first, n - 1, 2):
        if low - (step - 1) >= 0:
            pairs.append((low, low + 1))
        if low + step <= n - 1:
            pairs.append((low + 1, low))
    return pairs


def arrivals(n, c):
    order = []
    for step in range(1, n):
        from_right, from_left = c + step <= n - 1, c - step >= 0
        over = (from_right, from_left) if c % 2 == 0 else (from_left, from_right)
        order += [(links, step) for links in (0, 1) if over[links]]
    return order


def line_gather(shard, axis):
    n = lax.axis_size(axis)
    here = lax.axis_index(axis)
    came = {(0, 0): shard, (1, 0): shard}
    for step in range(1, n):
        for links in (0, 1):
            pairs = link_pairs(n, links, step)
            if pairs:
                came[links, step] = lax.ppermute(came[1 - links, step - 1], axis, pairs)
    slots, owners = [shard], [here]
    tables = [arrivals(n, c) for c in range(n)]
    for slot in range(n - 1):
        users = {}
        origins = []
        for c in range(n):
            links, step = tables[c][slot]
            users.setdefault((links, step), []).append(c)
            origins.append(c + step if links == c % 2 else c - step)
        choice = None
        for source, places in users.items():
            if choice is None:
                choice = came[source]
            else:
                mine = functools.reduce(jnp.logical_or, [here == c for c in places])
                choice = jnp.where(mine, came[source], choice)
        slots.append(choice)
        owners.append(jnp.array(origins, dtype=jnp.int32)[here])
    return slots, owners, came[0, 1]


def halving_sum(part, axis):
    n = lax.axis_size(axis)
    here = lax.axis_index(axis)
    bit = 1
    while bit < n:
        half = part.shape[-2] // 2
        high = (here // bit) % 2
        kept = lax.dynamic_slice_in_dim(part, high * half, half, axis=-2)
        sent = lax.dynamic_slice_in_dim(part, (1 - high) * half, half, axis=-2)
        came = lax.ppermute(sent, axis, [(i, i ^ bit) for i in range(n)])
        part = kept + came
        bit *= 2
    return part


def doubling_gather(part, axis):
    n = lax.axis_size(axis)
    here = lax.axis_index(axis)
    bit = n // 2
    while bit:
        came = lax.ppermute(part, axis, [(i, i ^ bit) for i in range(n)])
        part = jnp.where(
            (here // bit) % 2 == 1,
            jnp.concatenate([came, part], axis=-2),
            jnp.concatenate([part, came], axis=-2),
        )
        bit //= 2
    return part


def response_codes(logratio, token_session, token_position, pad_mask):
    live = pad_mask.astype(jnp.float32)
    response = (token_session * LIST + token_position).astype(jnp.float32)
    return jnp.stack([live * logratio, jnp.where(pad_mask != 0, response, -1.0)])


def coefficients(codes):
    n, _, rows = codes.shape
    onehot = (
        codes[:, 1, :, None] == jnp.arange(SESSIONS * LIST, dtype=jnp.float32)
    ).astype(jnp.float32)
    sums = jnp.sum(onehot * codes[:, 0, :, None], axis=(0, 1))
    scores = math.sqrt(SESSIONS * LIST / (n * rows)) * sums
    response_grad = listwise_grad(scores)
    return 0.1 * jnp.sum(onehot * response_grad, axis=2)


def on_device(
    tokens,
    out_grad,
    logratio,
    token_session,
    token_position,
    pad_mask,
    w_in,
    m_in,
    v_in,
    w_out,
    m_out,
    v_out,
):
    n = lax.axis_size("col")
    token_slots, owners, first = line_gather(tokens, "col")
    out_grad_slots, _, _ = line_gather(out_grad, "col")
    codes = response_codes(logratio, token_session, token_position, pad_mask)
    codes, _ = lax.optimization_barrier((codes, first))
    coeff = coefficients(lax.all_gather(codes, "col", axis=0))
    w_in16, w_out16 = lax.optimization_barrier(
        (w_in.astype(jnp.bfloat16), w_out.astype(jnp.bfloat16))
    )

    def scaled(slot):
        mine = lax.dynamic_index_in_dim(coeff, owners[slot], 0, keepdims=False)
        return (mine[:, None] * out_grad_slots[slot].astype(jnp.float32)).astype(jnp.bfloat16)

    def pre_of(slot):
        return jnp.dot(token_slots[slot], w_in16, preferred_element_type=jnp.float32)

    def square(pre):
        positive = jnp.maximum(pre, 0.0)
        return (positive * positive).astype(jnp.bfloat16)

    def chain(pre, back):
        return (back * 2.0 * jnp.maximum(pre, 0.0)).astype(jnp.bfloat16)

    early = range(n - 2)
    dys = [scaled(slot) for slot in range(n - 1)]
    sums = lax.psum([(pre_of(slot), against(dys[slot], w_out16)) for slot in early], "row")
    acts = [square(pre) for pre, _ in sums]
    dpres = [chain(pre, back) for pre, back in sums]
    both = halving_sum(jnp.stack([pre_of(n - 2), against(dys[n - 2], w_out16)]), "row")
    both = doubling_gather(jnp.stack([square(both[0]), chain(both[0], both[1])]), "row")
    acts.append(both[0])
    dpres.append(both[1])
    grad_in = grad_sum(token_slots[:-1], dpres, 256)
    grad_out = grad_sum(acts, dys, 128)

    pre = halving_sum(pre_of(n - 1), "row")
    act = doubling_gather(square(pre), "row")
    dy = scaled(n - 1)
    dy, grad_in, grad_out, act = lax.optimization_barrier((dy, grad_in, grad_out, act))
    back = halving_sum(against(dy, w_out16), "row")
    outs_out = update(act, dy, grad_out, w_out, m_out, v_out, 128)
    dpre = doubling_gather(chain(pre, back), "row")
    outs_in = update(token_slots[-1], dpre, grad_in, w_in, m_in, v_in, 256)
    return (*outs_in, *outs_out)


def solution(mesh):
    in_specs = (
        P("col", "row"),
        P("col", "row"),
        P("col"),
        P("col"),
        P("col"),
        P("col"),
        P("row", "col"),
        P("row", "col"),
        P("row", "col"),
        P("col", "row"),
        P("col", "row"),
        P("col", "row"),
    )
    out_specs = (
        P("row", "col"),
        P("row", "col"),
        P("row", "col"),
        P("col", "row"),
        P("col", "row"),
        P("col", "row"),
    )
    return jax.shard_map(
        on_device, mesh=mesh, in_specs=in_specs, out_specs=out_specs, check_vma=False
    )
```

```python
import functools
import math

import jax
import jax.numpy as jnp
from jax import lax
from jax.experimental import pallas as pl
from jax.experimental.pallas import tpu as pltpu
from jax.sharding import PartitionSpec as P

SESSIONS = 8
LIST = 4


def listwise_grad(scores):
    s = scores.reshape(SESSIONS, LIST)
    later = s[:, None, :] - s[:, :, None]
    order = jnp.arange(LIST)
    after = (order[None, :] > order[:, None]).astype(jnp.float32)
    before = (order[None, :] < order[:, None]).astype(jnp.float32)
    worse = -jnp.sum(after[None] * jax.nn.sigmoid(later), axis=2)
    better = jnp.sum(before[None] * jax.nn.sigmoid(-later), axis=2)
    return (worse + better).reshape(SESSIONS * LIST)


def adamw(weight, first, second, grad):
    new_first = 0.9 * first + 0.1 * grad
    new_second = 0.95 * second + 0.05 * (grad * grad)
    scaled = new_second * (1.0 / (1.0 - 0.95**20))
    below = scaled * lax.rsqrt(scaled) + 1e-08
    inverse = pl.reciprocal(below, approx=True)
    inverse = inverse * (2.0 - below * inverse)
    step = (0.0003 / (1.0 - 0.9**20)) * (new_first * inverse)
    return (weight * (1.0 - 0.0003 * 0.1) - step, new_first, new_second)


def over_rows(left, right):
    return lax.dot_general(
        left, right, (((0,), (0,)), ((), ())), preferred_element_type=jnp.float32
    )


def against(left, right):
    return lax.dot_general(
        left, right, (((1,), (1,)), ((), ())), preferred_element_type=jnp.float32
    )


def block_of(size, most):
    block = most
    while size % block:
        block -= 128
    return block


def grad_kernel(parts, *refs):
    lefts, rights, out = refs[:parts], refs[parts : 2 * parts], refs[2 * parts]
    total = over_rows(lefts[0][...], rights[0][...])
    for left, right in zip(lefts[1:], rights[1:]):
        total += over_rows(left[...], right[...])
    out[...] = total


def grad_sum(lefts, rights, most):
    rows, height = lefts[0].shape
    width = rights[0].shape[1]
    parts = len(lefts)
    block = block_of(height, most)
    return pl.pallas_call(
        functools.partial(grad_kernel, parts),
        grid=(height // block,),
        in_specs=[pl.BlockSpec((rows, block), lambda i: (0, i))] * parts
        + [pl.BlockSpec((rows, width), lambda i: (0, 0))] * parts,
        out_specs=pl.BlockSpec((block, width), lambda i: (i, 0)),
        out_shape=jax.ShapeDtypeStruct((height, width), jnp.float32),
        compiler_params=pltpu.CompilerParams(vmem_limit_bytes=44 * 2**20),
        cost_estimate=pl.CostEstimate(
            flops=2 * parts * rows * height * width,
            bytes_accessed=4 * height * width + 2 * parts * rows * (height + width),
            transcendentals=0,
        ),
    )(*lefts, *rights)


def update_kernel(left, right, grad, w, m, v, *refs):
    new_w, new_m, new_v = refs[-3:]
    total = grad[...] + over_rows(left[...], right[...])
    new_w[...], new_m[...], new_v[...] = adamw(w[...], m[...], v[...], total)


def update(left, right, grad, w, m, v, rows_most, part=0, parts=1, so_far=()):
    rows, height = left.shape
    width = right.shape[1] // parts
    block = block_of(height, rows_most)
    panel = pl.BlockSpec((block, width), lambda i: (i, part))
    shape = jax.ShapeDtypeStruct(w.shape, jnp.float32)
    return pl.pallas_call(
        update_kernel,
        grid=(height // block,),
        in_specs=[
            pl.BlockSpec((rows, block), lambda i: (0, i)),
            pl.BlockSpec((rows, width), lambda i: (0, part)),
            panel,
            panel,
            panel,
            panel,
        ]
        + [pl.BlockSpec(memory_space=pl.ANY)] * len(so_far),
        out_specs=[panel] * 3,
        out_shape=[shape] * 3,
        input_output_aliases={6 + i: i for i in range(len(so_far))},
        compiler_params=pltpu.CompilerParams(vmem_limit_bytes=56 * 2**20),
        cost_estimate=pl.CostEstimate(
            flops=2 * rows * height * width,
            bytes_accessed=7 * 4 * height * width + 2 * rows * (height + width),
            transcendentals=2 * height * width,
        ),
    )(left, right, grad, w, m, v, *so_far)


def link_pairs(n, first, step):
    pairs = []
    for low in range(first, n - 1, 2):
        if low - (step - 1) >= 0:
            pairs.append((low, low + 1))
        if low + step <= n - 1:
            pairs.append((low + 1, low))
    return pairs


def arrivals(n, c):
    order = []
    for step in range(1, n):
        from_right, from_left = c + step <= n - 1, c - step >= 0
        over = (from_right, from_left) if c % 2 == 0 else (from_left, from_right)
        order += [(links, step) for links in (0, 1) if over[links]]
    return order


def line_gather(shard, axis):
    n = lax.axis_size(axis)
    here = lax.axis_index(axis)
    came = {(0, 0): shard, (1, 0): shard}
    for step in range(1, n):
        for links in (0, 1):
            pairs = link_pairs(n, links, step)
            if pairs:
                came[links, step] = lax.ppermute(came[1 - links, step - 1], axis, pairs)
    slots, owners = [shard], [here]
    tables = [arrivals(n, c) for c in range(n)]
    for slot in range(n - 1):
        users = {}
        origins = []
        for c in range(n):
            links, step = tables[c][slot]
            users.setdefault((links, step), []).append(c)
            origins.append(c + step if links == c % 2 else c - step)
        choice = None
        for source, places in users.items():
            if choice is None:
                choice = came[source]
            else:
                mine = functools.reduce(jnp.logical_or, [here == c for c in places])
                choice = jnp.where(mine, came[source], choice)
        slots.append(choice)
        owners.append(jnp.array(origins, dtype=jnp.int32)[here])
    return slots, owners


def together(came, beside):
    if beside:
        came, _ = lax.optimization_barrier((came, beside.pop(0)()))
    return came


def halving_sum(part, axis, beside=None):
    n = lax.axis_size(axis)
    here = lax.axis_index(axis)
    bit = 1
    while bit < n:
        half = part.shape[-2] // 2
        high = (here // bit) % 2
        kept = lax.dynamic_slice_in_dim(part, high * half, half, axis=-2)
        sent = lax.dynamic_slice_in_dim(part, (1 - high) * half, half, axis=-2)
        came = lax.ppermute(sent, axis, [(i, i ^ bit) for i in range(n)])
        if bit > 1:
            came = together(came, beside)
        part = kept + came
        bit *= 2
    return part


def doubling_gather(part, axis, beside=None):
    n = lax.axis_size(axis)
    here = lax.axis_index(axis)
    bit = n // 2
    while bit:
        came = lax.ppermute(part, axis, [(i, i ^ bit) for i in range(n)])
        came = together(came, beside)
        part = jnp.where(
            (here // bit) % 2 == 1,
            jnp.concatenate([came, part], axis=-2),
            jnp.concatenate([part, came], axis=-2),
        )
        bit //= 2
    return part


def response_codes(logratio, token_session, token_position, pad_mask):
    live = pad_mask.astype(jnp.float32)
    response = (token_session * LIST + token_position).astype(jnp.float32)
    return jnp.stack([live * logratio, jnp.where(pad_mask != 0, response, -1.0)])


def coefficients(codes):
    n, _, rows = codes.shape
    onehot = (
        codes[:, 1, :, None] == jnp.arange(SESSIONS * LIST, dtype=jnp.float32)
    ).astype(jnp.float32)
    sums = jnp.sum(onehot * codes[:, 0, :, None], axis=(0, 1))
    scores = math.sqrt(SESSIONS * LIST / (n * rows)) * sums
    response_grad = listwise_grad(scores)
    return 0.1 * jnp.sum(onehot * response_grad, axis=2)


def on_device(
    tokens,
    out_grad,
    logratio,
    token_session,
    token_position,
    pad_mask,
    w_in,
    m_in,
    v_in,
    w_out,
    m_out,
    v_out,
):
    n = lax.axis_size("col")
    here = lax.axis_index("col")
    token_slots, owners = line_gather(tokens, "col")
    codes = response_codes(logratio, token_session, token_position, pad_mask)
    codes = jnp.stack(
        [codes]
        + [
            lax.ppermute(codes, "col", [(i, (i + shift) % n) for i in range(n)])
            for shift in range(1, n)
        ]
    )
    out_grad, codes = lax.optimization_barrier((out_grad, codes))
    out_grad_slots, _ = line_gather(out_grad, "col")
    coeff = coefficients(codes)
    w_in16, w_out16 = lax.optimization_barrier(
        (w_in.astype(jnp.bfloat16), w_out.astype(jnp.bfloat16))
    )

    def scaled(slot, after=None):
        shift = (here - owners[slot] + n) % n
        mine = lax.dynamic_index_in_dim(coeff, shift, 0, keepdims=False)
        if after is not None:
            mine, _ = lax.optimization_barrier((mine, after))
        return (mine[:, None] * out_grad_slots[slot].astype(jnp.float32)).astype(jnp.bfloat16)

    def pre_of(slot):
        return jnp.dot(token_slots[slot], w_in16, preferred_element_type=jnp.float32)

    def square(pre):
        positive = jnp.maximum(pre, 0.0)
        return (positive * positive).astype(jnp.bfloat16)

    def chain(pre, back):
        return (back * 2.0 * jnp.maximum(pre, 0.0)).astype(jnp.bfloat16)

    early = range(n - 2)
    dys = [scaled(slot) for slot in range(n - 1)]
    sums = lax.psum([(pre_of(slot), against(dys[slot], w_out16)) for slot in early], "row")
    both = halving_sum(jnp.stack([pre_of(n - 2), against(dys[n - 2], w_out16)]), "row")
    both = doubling_gather(jnp.stack([square(both[0]), chain(both[0], both[1])]), "row")
    sums, both = lax.optimization_barrier((sums, both))
    acts = [square(pre) for pre, _ in sums] + [both[0]]
    dpres = [chain(pre, back) for pre, back in sums] + [both[1]]
    grad_in = grad_sum(token_slots[:-1], dpres, 256)
    grad_out = grad_sum(acts, dys, 128)

    pre = halving_sum(pre_of(n - 1), "row")
    act = doubling_gather(square(pre), "row")
    dy = scaled(n - 1, (grad_in, grad_out, act))
    parts = 3
    outs_out = ()

    def update_part(part):
        def run():
            nonlocal outs_out
            outs_out = update(
                act, dy, grad_out, w_out, m_out, v_out, 256, part, parts, outs_out
            )
            return outs_out

        return run

    beside = [update_part(part) for part in range(parts)]
    back = halving_sum(against(dy, w_out16), "row", beside)
    dpre = doubling_gather(chain(pre, back), "row", beside)
    while beside:
        beside.pop(0)()
    outs_in = update(token_slots[-1], dpre, grad_in, w_in, m_in, v_in, 256)
    return (*outs_in, *outs_out)


def solution(mesh):
    in_specs = (
        P("col", "row"),
        P("col", "row"),
        P("col"),
        P("col"),
        P("col"),
        P("col"),
        P("row", "col"),
        P("row", "col"),
        P("row", "col"),
        P("col", "row"),
        P("col", "row"),
        P("col", "row"),
    )
    out_specs = (
        P("row", "col"),
        P("row", "col"),
        P("row", "col"),
        P("col", "row"),
        P("col", "row"),
        P("col", "row"),
    )
    return jax.shard_map(
        on_device, mesh=mesh, in_specs=in_specs, out_specs=out_specs, check_vma=False
    )
```

```python
import functools
import math

import jax
import jax.numpy as jnp
from jax import lax
from jax.experimental import pallas as pl
from jax.experimental.pallas import tpu as pltpu
from jax.sharding import PartitionSpec as P

SESSIONS = 8
LIST = 4


def listwise_grad(scores):
    s = scores.reshape(SESSIONS, LIST)
    later = s[:, None, :] - s[:, :, None]
    order = jnp.arange(LIST)
    after = (order[None, :] > order[:, None]).astype(jnp.float32)
    before = (order[None, :] < order[:, None]).astype(jnp.float32)
    worse = -jnp.sum(after[None] * jax.nn.sigmoid(later), axis=2)
    better = jnp.sum(before[None] * jax.nn.sigmoid(-later), axis=2)
    return (worse + better).reshape(SESSIONS * LIST)


def adamw(weight, first, second, grad):
    new_first = 0.9 * first + 0.1 * grad
    new_second = 0.95 * second + 0.05 * (grad * grad)
    scaled = new_second * (1.0 / (1.0 - 0.95**20))
    below = scaled * lax.rsqrt(scaled) + 1e-08
    inverse = pl.reciprocal(below, approx=True)
    inverse = inverse * (2.0 - below * inverse)
    step = (0.0003 / (1.0 - 0.9**20)) * (new_first * inverse)
    return (weight * (1.0 - 0.0003 * 0.1) - step, new_first, new_second)


def over_rows(left, right):
    return lax.dot_general(
        left, right, (((0,), (0,)), ((), ())), preferred_element_type=jnp.float32
    )


def against(left, right):
    return lax.dot_general(
        left, right, (((1,), (1,)), ((), ())), preferred_element_type=jnp.float32
    )


def block_of(size, most):
    block = most
    while size % block:
        block -= 128
    return block


def grad_kernel(parts, *refs):
    lefts, rights, out = refs[:parts], refs[parts : 2 * parts], refs[2 * parts]
    total = over_rows(lefts[0][...], rights[0][...])
    for left, right in zip(lefts[1:], rights[1:]):
        total += over_rows(left[...], right[...])
    out[...] = total


def grad_sum(lefts, rights, most):
    rows, height = lefts[0].shape
    width = rights[0].shape[1]
    parts = len(lefts)
    block = block_of(height, most)
    return pl.pallas_call(
        functools.partial(grad_kernel, parts),
        grid=(height // block,),
        in_specs=[pl.BlockSpec((rows, block), lambda i: (0, i))] * parts
        + [pl.BlockSpec((rows, width), lambda i: (0, 0))] * parts,
        out_specs=pl.BlockSpec((block, width), lambda i: (i, 0)),
        out_shape=jax.ShapeDtypeStruct((height, width), jnp.float32),
        compiler_params=pltpu.CompilerParams(vmem_limit_bytes=44 * 2**20),
        cost_estimate=pl.CostEstimate(
            flops=2 * parts * rows * height * width,
            bytes_accessed=4 * height * width + 2 * parts * rows * (height + width),
            transcendentals=0,
        ),
    )(*lefts, *rights)


def update_kernel(shards, *refs):
    lefts, rights = refs[:shards], refs[shards : 2 * shards]
    grad, w, m, v = refs[2 * shards : 2 * shards + 4]
    new_w, new_m, new_v, total = refs[-4:]
    summed = grad[...]
    for left, right in zip(lefts, rights):
        summed += over_rows(left[...], right[...])
    total[...] = summed

    def eight_rows(i, carry):
        rows = pl.ds(pl.multiple_of(8 * i, 8), 8)
        new_w[rows, :], new_m[rows, :], new_v[rows, :] = adamw(
            w[rows, :], m[rows, :], v[rows, :], total[rows, :]
        )
        return carry

    lax.fori_loop(0, total.shape[0] // 8, eight_rows, 0, unroll=2)


def update(lefts, rights, grad, w, m, v, most, part=0, parts=1, so_far=()):
    shards = len(lefts)
    rows, height = lefts[0].shape
    width = rights[0].shape[1] // parts
    block = block_of(height, most)
    panel = pl.BlockSpec((block, width), lambda i: (i, part))
    shape = jax.ShapeDtypeStruct(w.shape, jnp.float32)
    return pl.pallas_call(
        functools.partial(update_kernel, shards),
        grid=(height // block,),
        in_specs=[pl.BlockSpec((rows, block), lambda i: (0, i))] * shards
        + [pl.BlockSpec((rows, width), lambda i: (0, part))] * shards
        + [panel] * 4
        + [pl.BlockSpec(memory_space=pl.ANY)] * len(so_far),
        out_specs=[panel] * 3,
        out_shape=[shape] * 3,
        scratch_shapes=[pltpu.VMEM((block, width), jnp.float32)],
        input_output_aliases={2 * shards + 4 + i: i for i in range(len(so_far))},
        compiler_params=pltpu.CompilerParams(vmem_limit_bytes=56 * 2**20),
        cost_estimate=pl.CostEstimate(
            flops=2 * shards * rows * height * width,
            bytes_accessed=7 * 4 * height * width + 2 * shards * rows * (height + width),
            transcendentals=2 * height * width,
        ),
    )(*lefts, *rights, grad, w, m, v, *so_far)


def link_pairs(n, first, step):
    pairs = []
    for low in range(first, n - 1, 2):
        if low - (step - 1) >= 0:
            pairs.append((low, low + 1))
        if low + step <= n - 1:
            pairs.append((low + 1, low))
    return pairs


def arrivals(n, c):
    order = []
    for step in range(1, n):
        from_right, from_left = c + step <= n - 1, c - step >= 0
        over = (from_right, from_left) if c % 2 == 0 else (from_left, from_right)
        order += [(links, step) for links in (0, 1) if over[links]]
    return order


def line_gather(shard, axis):
    n = lax.axis_size(axis)
    here = lax.axis_index(axis)
    came = {(0, 0): shard, (1, 0): shard}
    for step in range(1, n):
        arrived = {}
        for links in (0, 1):
            pairs = link_pairs(n, links, step)
            if pairs:
                arrived[links, step] = lax.ppermute(came[1 - links, step - 1], axis, pairs)
        came.update(lax.optimization_barrier(arrived))
    slots, owners = [shard], [here]
    tables = [arrivals(n, c) for c in range(n)]
    for slot in range(n - 1):
        users = {}
        origins = []
        for c in range(n):
            links, step = tables[c][slot]
            users.setdefault((links, step), []).append(c)
            origins.append(c + step if links == c % 2 else c - step)
        choice = None
        for source, places in users.items():
            if choice is None:
                choice = came[source]
            else:
                mine = functools.reduce(jnp.logical_or, [here == c for c in places])
                choice = jnp.where(mine, came[source], choice)
        slots.append(choice)
        owners.append(jnp.array(origins, dtype=jnp.int32)[here])
    return slots, owners


def after(value, earlier):
    if earlier is not None:
        value, _ = lax.optimization_barrier((value, earlier))
    return value


def exchange(part, axis, mask, beside=None):
    came = lax.ppermute(part, axis, [(i, i ^ mask) for i in range(lax.axis_size(axis))])
    work = beside.pop(0) if beside else None
    return after(came, work() if callable(work) else work)


def row_sum(part, axis, beside=None):
    here = lax.axis_index(axis)
    others = lax.axis_size(axis) // 2
    half = part.shape[0] // 2
    odd, place = here % 2, here // 2
    kept = lax.dynamic_slice_in_dim(part, odd * half, half)
    sent = lax.dynamic_slice_in_dim(part, (1 - odd) * half, half)
    part = kept + exchange(sent, axis, 1, beside)
    piece = half // others
    total = lax.dynamic_slice_in_dim(part, place * piece, piece)
    came = [
        exchange(lax.dynamic_slice_in_dim(part, (place ^ other) * piece, piece), axis, 2 * other)
        for other in range(1, others)
    ]
    work = beside.pop(0) if beside else None
    came = after(came, work() if callable(work) else work)
    return functools.reduce(jnp.add, came, total)


def row_gather(part, axis, beside=None):
    here = lax.axis_index(axis)
    others = lax.axis_size(axis) // 2
    odd, place = here % 2, here // 2
    pieces = [part] + [exchange(part, axis, 2 * other) for other in range(1, others)]
    work = beside.pop(0) if beside else None
    pieces = after(pieces, work() if callable(work) else work)
    bit = 1
    while bit < others:
        pieces = [
            jnp.where((place // bit) % 2 == 1, pieces[i ^ bit], pieces[i]) for i in range(others)
        ]
        bit *= 2
    part = jnp.concatenate(pieces)
    came = exchange(part, axis, 1, beside)
    return jnp.where(
        odd == 1, jnp.concatenate([came, part]), jnp.concatenate([part, came])
    )


def response_codes(logratio, token_session, token_position, pad_mask):
    live = pad_mask.astype(jnp.float32)
    response = (token_session * LIST + token_position).astype(jnp.float32)
    return jnp.stack([live * logratio, jnp.where(pad_mask != 0, response, -1.0)])


def coefficients(codes):
    n, _, rows = codes.shape
    onehot = (
        codes[:, 1, :, None] == jnp.arange(SESSIONS * LIST, dtype=jnp.float32)
    ).astype(jnp.float32)
    sums = jnp.sum(onehot * codes[:, 0, :, None], axis=(0, 1))
    scores = math.sqrt(SESSIONS * LIST / (n * rows)) * sums
    response_grad = listwise_grad(scores)
    return 0.1 * jnp.sum(onehot * response_grad, axis=2)


def on_device(
    tokens,
    out_grad,
    logratio,
    token_session,
    token_position,
    pad_mask,
    w_in,
    m_in,
    v_in,
    w_out,
    m_out,
    v_out,
):
    n = lax.axis_size("col")
    here = lax.axis_index("col")
    codes = response_codes(logratio, token_session, token_position, pad_mask)
    codes = jnp.stack(
        [codes]
        + [
            lax.ppermute(codes, "col", [(i, (i + shift) % n) for i in range(n)])
            for shift in range(1, n)
        ]
    )
    out_grad, codes = lax.optimization_barrier((out_grad, codes))
    coeff = coefficients(codes)
    w_in16, w_out16 = lax.optimization_barrier(
        (w_in.astype(jnp.bfloat16), w_out.astype(jnp.bfloat16))
    )

    def scaled(shard, owner, earlier=None):
        mine = lax.dynamic_index_in_dim(coeff, (here - owner + n) % n, 0, keepdims=False)
        mine = after(mine, earlier)
        return (mine[:, None] * shard.astype(jnp.float32)).astype(jnp.bfloat16)

    def pre_of(shard):
        return jnp.dot(shard, w_in16, preferred_element_type=jnp.float32)

    def square(pre):
        positive = jnp.maximum(pre, 0.0)
        return (positive * positive).astype(jnp.bfloat16)

    def chain(pre, back):
        return (back * 2.0 * jnp.maximum(pre, 0.0)).astype(jnp.bfloat16)

    token_slots, owners = line_gather(tokens, "col")
    out_grad_slots, _ = line_gather(out_grad, "col")
    parts = 3
    outs_out = ()

    def update_part(part):
        def run():
            nonlocal outs_out
            outs_out = update(
                acts[-2:], dys[-2:], grad_out, w_out, m_out, v_out, 128, part, parts, outs_out
            )
            return outs_out

        return run

    waits = [x for pair in zip(token_slots[1:], out_grad_slots[1:]) for x in pair][:-1]
    acts, dpres, dys = [], [], []
    last = None
    for slot in range(n):
        pre = row_sum(after(pre_of(token_slots[slot]), last), "row")
        latest = [out_grad_slots[n - 1]] if slot == n - 1 else None
        acts.append(row_gather(square(pre), "row", latest))
        if slot == n - 1:
            break
        last = (acts[-1], waits.pop(0))
        dys.append(scaled(out_grad_slots[slot], owners[slot]))
        back = row_sum(after(against(dys[slot], w_out16), last), "row")
        dpres.append(row_gather(chain(pre, back), "row"))
        last = (dpres[-1], waits.pop(0) if waits else ())

    grad_in = grad_sum(token_slots[:-2], dpres[:-1], 256)
    grad_out = grad_sum(acts[:-2], dys[:-1], 128)

    dys.append(scaled(out_grad_slots[n - 1], owners[n - 1], (grad_in, grad_out, acts)))
    work = [None] + [update_part(part) for part in range(parts)]
    back = row_sum(against(dys[n - 1], w_out16), "row", work)
    dpres.append(row_gather(chain(pre, back), "row", work))
    while work:
        work.pop(0)()
    outs_in = update(token_slots[-2:], dpres[-2:], grad_in, w_in, m_in, v_in, 128)
    return (*outs_in, *outs_out)


def solution(mesh):
    in_specs = (
        P("col", "row"),
        P("col", "row"),
        P("col"),
        P("col"),
        P("col"),
        P("col"),
        P("row", "col"),
        P("row", "col"),
        P("row", "col"),
        P("col", "row"),
        P("col", "row"),
        P("col", "row"),
    )
    out_specs = (
        P("row", "col"),
        P("row", "col"),
        P("row", "col"),
        P("col", "row"),
        P("col", "row"),
        P("col", "row"),
    )
    return jax.shard_map(
        on_device, mesh=mesh, in_specs=in_specs, out_specs=out_specs, check_vma=False
    )
```

```python
import functools
import math

import jax
import jax.numpy as jnp
from jax import lax
from jax.experimental import pallas as pl
from jax.experimental.pallas import tpu as pltpu
from jax.sharding import PartitionSpec as P

SESSIONS = 8
LIST = 4


def listwise_grad(scores):
    s = scores.reshape(SESSIONS, LIST)
    later = s[:, None, :] - s[:, :, None]
    order = jnp.arange(LIST)
    after = (order[None, :] > order[:, None]).astype(jnp.float32)
    before = (order[None, :] < order[:, None]).astype(jnp.float32)
    worse = -jnp.sum(after[None] * jax.nn.sigmoid(later), axis=2)
    better = jnp.sum(before[None] * jax.nn.sigmoid(-later), axis=2)
    return (worse + better).reshape(SESSIONS * LIST)


def adamw(weight, first, second, grad):
    new_first = 0.9 * first + 0.1 * grad
    new_second = 0.95 * second + 0.05 * (grad * grad)
    scaled = new_second * (1.0 / (1.0 - 0.95**20))
    below = scaled * lax.rsqrt(scaled) + 1e-08
    inverse = pl.reciprocal(below, approx=True)
    inverse = inverse * (2.0 - below * inverse)
    step = (0.0003 / (1.0 - 0.9**20)) * (new_first * inverse)
    return (weight * (1.0 - 0.0003 * 0.1) - step, new_first, new_second)


def over_rows(left, right):
    return lax.dot_general(
        left, right, (((0,), (0,)), ((), ())), preferred_element_type=jnp.float32
    )


def against(left, right):
    return lax.dot_general(
        left, right, (((1,), (1,)), ((), ())), preferred_element_type=jnp.float32
    )


def block_of(size, most):
    block = most
    while size % block:
        block -= 128
    return block


def grad_kernel(parts, *refs):
    lefts, rights, out = refs[:parts], refs[parts : 2 * parts], refs[2 * parts]
    total = over_rows(lefts[0][...], rights[0][...])
    for left, right in zip(lefts[1:], rights[1:]):
        total += over_rows(left[...], right[...])
    out[...] = total


def grad_sum(lefts, rights, most):
    rows, height = lefts[0].shape
    width = rights[0].shape[1]
    parts = len(lefts)
    block = block_of(height, most)
    return pl.pallas_call(
        functools.partial(grad_kernel, parts),
        grid=(height // block,),
        in_specs=[pl.BlockSpec((rows, block), lambda i: (0, i))] * parts
        + [pl.BlockSpec((rows, width), lambda i: (0, 0))] * parts,
        out_specs=pl.BlockSpec((block, width), lambda i: (i, 0)),
        out_shape=jax.ShapeDtypeStruct((height, width), jnp.float32),
        compiler_params=pltpu.CompilerParams(vmem_limit_bytes=44 * 2**20),
        cost_estimate=pl.CostEstimate(
            flops=2 * parts * rows * height * width,
            bytes_accessed=4 * height * width + 2 * parts * rows * (height + width),
            transcendentals=0,
        ),
    )(*lefts, *rights)


def update_kernel(left, right, grad, w, m, v, *refs):
    new_w, new_m, new_v = refs[-3:]
    total = grad[...] + over_rows(left[...], right[...])
    new_w[...], new_m[...], new_v[...] = adamw(w[...], m[...], v[...], total)


def update(left, right, grad, w, m, v, most, part=0, parts=1, so_far=()):
    rows, height = left.shape
    width = right.shape[1] // parts
    block = block_of(height, most)
    panel = pl.BlockSpec((block, width), lambda i: (i, part))
    shape = jax.ShapeDtypeStruct(w.shape, jnp.float32)
    return pl.pallas_call(
        update_kernel,
        grid=(height // block,),
        in_specs=[
            pl.BlockSpec((rows, block), lambda i: (0, i)),
            pl.BlockSpec((rows, width), lambda i: (0, part)),
        ]
        + [panel] * 4
        + [pl.BlockSpec(memory_space=pl.ANY)] * len(so_far),
        out_specs=[panel] * 3,
        out_shape=[shape] * 3,
        input_output_aliases={6 + i: i for i in range(len(so_far))},
        compiler_params=pltpu.CompilerParams(vmem_limit_bytes=56 * 2**20),
        cost_estimate=pl.CostEstimate(
            flops=2 * rows * height * width,
            bytes_accessed=7 * 4 * height * width + 2 * rows * (height + width),
            transcendentals=2 * height * width,
        ),
    )(left, right, grad, w, m, v, *so_far)


def link_pairs(n, first, step):
    pairs = []
    for low in range(first, n - 1, 2):
        if low - (step - 1) >= 0:
            pairs.append((low, low + 1))
        if low + step <= n - 1:
            pairs.append((low + 1, low))
    return pairs


def arrivals(n, c):
    order = []
    for step in range(1, n):
        from_right, from_left = c + step <= n - 1, c - step >= 0
        over = (from_right, from_left) if c % 2 == 0 else (from_left, from_right)
        order += [(links, step) for links in (0, 1) if over[links]]
    return order


def line_gather(shard, axis):
    n = lax.axis_size(axis)
    here = lax.axis_index(axis)
    came = {(0, 0): shard, (1, 0): shard}
    for step in range(1, n):
        arrived = {}
        for links in (0, 1):
            pairs = link_pairs(n, links, step)
            if pairs:
                arrived[links, step] = lax.ppermute(came[1 - links, step - 1], axis, pairs)
        came.update(lax.optimization_barrier(arrived))
    slots, owners = [shard], [here]
    tables = [arrivals(n, c) for c in range(n)]
    for slot in range(n - 1):
        users = {}
        origins = []
        for c in range(n):
            links, step = tables[c][slot]
            users.setdefault((links, step), []).append(c)
            origins.append(c + step if links == c % 2 else c - step)
        choice = None
        for source, places in users.items():
            if choice is None:
                choice = came[source]
            else:
                mine = functools.reduce(jnp.logical_or, [here == c for c in places])
                choice = jnp.where(mine, came[source], choice)
        slots.append(choice)
        owners.append(jnp.array(origins, dtype=jnp.int32)[here])
    return slots, owners, [[came[at] for at in came if at[1] == step] for step in range(n)]


def after(value, earlier):
    if earlier is not None:
        value, _ = lax.optimization_barrier((value, earlier))
    return value


def exchange(part, axis, mask, beside=None):
    came = lax.ppermute(part, axis, [(i, i ^ mask) for i in range(lax.axis_size(axis))])
    work = beside.pop(0) if beside else None
    return after(came, work() if callable(work) else work)


def row_sum(part, axis, beside=None):
    here = lax.axis_index(axis)
    others = lax.axis_size(axis) // 2
    half = part.shape[-2] // 2
    odd, place = here % 2, here // 2
    kept = lax.dynamic_slice_in_dim(part, odd * half, half, axis=-2)
    sent = lax.dynamic_slice_in_dim(part, (1 - odd) * half, half, axis=-2)
    part = kept + exchange(sent, axis, 1, beside)
    piece = half // others

    def piece_of(which):
        return lax.dynamic_slice_in_dim(part, which * piece, piece, axis=-2)

    came = [exchange(piece_of(place ^ d), axis, 2 * d) for d in range(1, others)]
    work = beside.pop(0) if beside else None
    came = after(came, work() if callable(work) else work)
    return functools.reduce(jnp.add, came, piece_of(place))


def row_gather(part, axis, beside=None):
    here = lax.axis_index(axis)
    others = lax.axis_size(axis) // 2
    odd, place = here % 2, here // 2
    pieces = [part] + [exchange(part, axis, 2 * d) for d in range(1, others)]
    work = beside.pop(0) if beside else None
    pieces = after(pieces, work() if callable(work) else work)
    bit = 1
    while bit < others:
        pieces = [
            jnp.where((place // bit) % 2 == 1, pieces[i ^ bit], pieces[i]) for i in range(others)
        ]
        bit *= 2
    part = jnp.concatenate(pieces, axis=-2)
    came = exchange(part, axis, 1, beside)
    return jnp.where(
        odd == 1,
        jnp.concatenate([came, part], axis=-2),
        jnp.concatenate([part, came], axis=-2),
    )


def response_codes(logratio, token_session, token_position, pad_mask):
    live = pad_mask.astype(jnp.float32)
    response = (token_session * LIST + token_position).astype(jnp.float32)
    return jnp.stack([live * logratio, jnp.where(pad_mask != 0, response, -1.0)])


def coefficients(codes):
    n, _, rows = codes.shape
    onehot = (
        codes[:, 1, :, None] == jnp.arange(SESSIONS * LIST, dtype=jnp.float32)
    ).astype(jnp.float32)
    sums = jnp.sum(onehot * codes[:, 0, :, None], axis=(0, 1))
    scores = math.sqrt(SESSIONS * LIST / (n * rows)) * sums
    response_grad = listwise_grad(scores)
    return 0.1 * jnp.sum(onehot * response_grad, axis=2)


def on_device(
    tokens,
    out_grad,
    logratio,
    token_session,
    token_position,
    pad_mask,
    w_in,
    m_in,
    v_in,
    w_out,
    m_out,
    v_out,
):
    n = lax.axis_size("col")
    here = lax.axis_index("col")
    codes = response_codes(logratio, token_session, token_position, pad_mask)
    codes = jnp.stack(
        [codes]
        + [
            lax.ppermute(codes, "col", [(i, (i + shift) % n) for i in range(n)])
            for shift in range(1, n)
        ]
    )
    out_grad, codes = lax.optimization_barrier((out_grad, codes))
    coeff = coefficients(codes)
    w_in16, w_out16 = lax.optimization_barrier(
        (w_in.astype(jnp.bfloat16), w_out.astype(jnp.bfloat16))
    )

    def scaled(shard, owner, earlier=None):
        mine = lax.dynamic_index_in_dim(coeff, (here - owner + n) % n, 0, keepdims=False)
        mine = after(mine, earlier)
        return (mine[:, None] * shard.astype(jnp.float32)).astype(jnp.bfloat16)

    def pre_of(shard):
        return jnp.dot(shard, w_in16, preferred_element_type=jnp.float32)

    def square(pre):
        positive = jnp.maximum(pre, 0.0)
        return (positive * positive).astype(jnp.bfloat16)

    def chain(pre, back):
        return (back * 2.0 * jnp.maximum(pre, 0.0)).astype(jnp.bfloat16)

    token_slots, owners, tokens_came = line_gather(tokens, "col")
    out_grad_slots, _, out_grads_came = line_gather(out_grad, "col")
    parts = next(p for p in (2, 3, 1) if w_out.shape[1] % (128 * p) == 0)
    outs_out = ()

    def update_part(part):
        def run():
            nonlocal outs_out
            outs_out = update(
                acts[-1], dys[-1], grad_out, w_out, m_out, v_out, 128, part, parts, outs_out
            )
            return outs_out

        return run

    dys = [scaled(out_grad, here)]
    pre = row_sum(pre_of(tokens), "row")
    acts, dpres = [row_gather(square(pre), "row")], []
    both = jnp.stack([against(dys[0], w_out16), pre_of(token_slots[1])])
    both = row_sum(after(both, (acts[0], tokens_came[1])), "row")
    both, pre = jnp.stack([chain(pre, both[0]), square(both[1])]), both[1]
    last = both = row_gather(both, "row")
    acts.append(both[1])
    dpres.append(both[0])
    for slot in range(1, n):
        if slot > 1:
            last = (last, tokens_came[slot])
            beside, latest = None, None
            if slot == n - 1:
                grad_in = grad_sum(token_slots[:-1], dpres, 256)
                grad_out = grad_sum(acts, dys, 128)
                beside, latest = [None, (grad_in, grad_out)], [out_grads_came[slot]]
            pre = row_sum(after(pre_of(token_slots[slot]), last), "row", beside)
            last = row_gather(square(pre), "row", latest)
            acts.append(last)
        if slot < n - 1:
            dys.append(scaled(out_grad_slots[slot], owners[slot]))
            back = after(against(dys[slot], w_out16), (last, out_grads_came[slot]))
            last = row_gather(chain(pre, row_sum(back, "row")), "row")
            dpres.append(last)

    dys.append(scaled(out_grad_slots[n - 1], owners[n - 1], acts[-1]))
    work = [None] + [update_part(part) for part in range(parts)]
    back = row_sum(against(dys[n - 1], w_out16), "row", work)
    dpres.append(row_gather(chain(pre, back), "row", work))
    while work:
        work.pop(0)()
    outs_in = update(token_slots[-1], dpres[-1], grad_in, w_in, m_in, v_in, 256)
    return (*outs_in, *outs_out)


def solution(mesh):
    in_specs = (
        P("col", "row"),
        P("col", "row"),
        P("col"),
        P("col"),
        P("col"),
        P("col"),
        P("row", "col"),
        P("row", "col"),
        P("row", "col"),
        P("col", "row"),
        P("col", "row"),
        P("col", "row"),
    )
    out_specs = (
        P("row", "col"),
        P("row", "col"),
        P("row", "col"),
        P("col", "row"),
        P("col", "row"),
        P("col", "row"),
    )
    return jax.shard_map(
        on_device, mesh=mesh, in_specs=in_specs, out_specs=out_specs, check_vma=False
    )
```

```python
import functools
import math

import jax
import jax.numpy as jnp
from jax import lax
from jax.experimental import pallas as pl
from jax.experimental.pallas import tpu as pltpu
from jax.sharding import PartitionSpec as P

SESSIONS = 8
LIST = 4


def listwise_grad(scores):
    s = scores.reshape(SESSIONS, LIST)
    later = s[:, None, :] - s[:, :, None]
    order = jnp.arange(LIST)
    after = (order[None, :] > order[:, None]).astype(jnp.float32)
    before = (order[None, :] < order[:, None]).astype(jnp.float32)
    worse = -jnp.sum(after[None] * jax.nn.sigmoid(later), axis=2)
    better = jnp.sum(before[None] * jax.nn.sigmoid(-later), axis=2)
    return (worse + better).reshape(SESSIONS * LIST)


def adamw(weight, first, second, grad):
    new_first = 0.9 * first + 0.1 * grad
    new_second = 0.95 * second + 0.05 * (grad * grad)
    scaled = new_second * (1.0 / (1.0 - 0.95**20))
    below = scaled * lax.rsqrt(scaled) + 1e-08
    inverse = pl.reciprocal(below, approx=True)
    inverse = inverse * (2.0 - below * inverse)
    step = (0.0003 / (1.0 - 0.9**20)) * (new_first * inverse)
    return (weight * (1.0 - 0.0003 * 0.1) - step, new_first, new_second)


def over_rows(left, right):
    return lax.dot_general(
        left, right, (((0,), (0,)), ((), ())), preferred_element_type=jnp.float32
    )


def against(left, right):
    return lax.dot_general(
        left, right, (((1,), (1,)), ((), ())), preferred_element_type=jnp.float32
    )


def block_of(size, most):
    block = most
    while size % block:
        block -= 128
    return block


def grad_kernel(parts, *refs):
    lefts, rights, out = refs[:parts], refs[parts : 2 * parts], refs[2 * parts]
    total = over_rows(lefts[0][...], rights[0][...])
    for left, right in zip(lefts[1:], rights[1:]):
        total += over_rows(left[...], right[...])
    out[...] = total


def grad_sum(lefts, rights, most):
    rows, height = lefts[0].shape
    width = rights[0].shape[1]
    parts = len(lefts)
    block = block_of(height, most)
    return pl.pallas_call(
        functools.partial(grad_kernel, parts),
        grid=(height // block,),
        in_specs=[pl.BlockSpec((rows, block), lambda i: (0, i))] * parts
        + [pl.BlockSpec((rows, width), lambda i: (0, 0))] * parts,
        out_specs=pl.BlockSpec((block, width), lambda i: (i, 0)),
        out_shape=jax.ShapeDtypeStruct((height, width), jnp.float32),
        compiler_params=pltpu.CompilerParams(vmem_limit_bytes=44 * 2**20),
        cost_estimate=pl.CostEstimate(
            flops=2 * parts * rows * height * width,
            bytes_accessed=4 * height * width + 2 * parts * rows * (height + width),
            transcendentals=0,
        ),
    )(*lefts, *rights)


def update_kernel(shards, *refs):
    lefts, rights = refs[:shards], refs[shards : 2 * shards]
    grad, w, m, v = refs[2 * shards : 2 * shards + 4]
    new_w, new_m, new_v, late = refs[-4:]
    height = lefts[0].shape[1]
    block = w.shape[0]
    step = pl.program_id(0)

    @pl.when(step == 0)
    def _():
        span = block_of(height, 768)
        for at in range(0, height, span):
            columns = slice(at, at + span)
            total = over_rows(lefts[0][:, columns], rights[0][...])
            for left, right in zip(lefts[1:], rights[1:]):
                total += over_rows(left[:, columns], right[...])
            late[columns, :] = total

    def some_rows(i, carry):
        rows = pl.ds(pl.multiple_of(16 * i, 16), 16)
        late_rows = pl.ds(pl.multiple_of(step * block + 16 * i, 16), 16)
        new_w[rows, :], new_m[rows, :], new_v[rows, :] = adamw(
            w[rows, :], m[rows, :], v[rows, :], grad[rows, :] + late[late_rows, :]
        )
        return carry

    lax.fori_loop(0, block // 16, some_rows, 0, unroll=4)


def update(lefts, rights, grad, w, m, v, most, part=0, parts=1, so_far=()):
    shards = len(lefts)
    rows, height = lefts[0].shape
    width = rights[0].shape[1] // parts
    block = block_of(height, most)
    panel = pl.BlockSpec((block, width), lambda i: (i, part))
    shape = jax.ShapeDtypeStruct(w.shape, jnp.float32)
    return pl.pallas_call(
        functools.partial(update_kernel, shards),
        grid=(height // block,),
        in_specs=[pl.BlockSpec((rows, height), lambda i: (0, 0))] * shards
        + [pl.BlockSpec((rows, width), lambda i: (0, part))] * shards
        + [panel] * 4
        + [pl.BlockSpec(memory_space=pl.ANY)] * len(so_far),
        out_specs=[panel] * 3,
        out_shape=[shape] * 3,
        scratch_shapes=[pltpu.VMEM((height, width), jnp.float32)],
        input_output_aliases={2 * shards + 4 + i: i for i in range(len(so_far))},
        compiler_params=pltpu.CompilerParams(vmem_limit_bytes=56 * 2**20),
        cost_estimate=pl.CostEstimate(
            flops=2 * shards * rows * height * width,
            bytes_accessed=7 * 4 * height * width + 2 * shards * rows * (height + width),
            transcendentals=2 * height * width,
        ),
    )(*lefts, *rights, grad, w, m, v, *so_far)


def link_pairs(n, first, step):
    pairs = []
    for low in range(first, n - 1, 2):
        if low - (step - 1) >= 0:
            pairs.append((low, low + 1))
        if low + step <= n - 1:
            pairs.append((low + 1, low))
    return pairs


def arrivals(n, c):
    order = []
    for step in range(1, n):
        from_right, from_left = c + step <= n - 1, c - step >= 0
        over = (from_right, from_left) if c % 2 == 0 else (from_left, from_right)
        order += [(links, step) for links in (0, 1) if over[links]]
    return order


def line_gather(shard, axis):
    n = lax.axis_size(axis)
    here = lax.axis_index(axis)
    came = {(0, 0): shard, (1, 0): shard}
    for step in range(1, n):
        arrived = {}
        for links in (0, 1):
            pairs = link_pairs(n, links, step)
            if pairs:
                arrived[links, step] = lax.ppermute(came[1 - links, step - 1], axis, pairs)
        came.update(lax.optimization_barrier(arrived))
    slots, owners = [shard], [here]
    tables = [arrivals(n, c) for c in range(n)]
    for slot in range(n - 1):
        users = {}
        origins = []
        for c in range(n):
            links, step = tables[c][slot]
            users.setdefault((links, step), []).append(c)
            origins.append(c + step if links == c % 2 else c - step)
        choice = None
        for source, places in users.items():
            if choice is None:
                choice = came[source]
            else:
                mine = functools.reduce(jnp.logical_or, [here == c for c in places])
                choice = jnp.where(mine, came[source], choice)
        slots.append(choice)
        owners.append(jnp.array(origins, dtype=jnp.int32)[here])
    return slots, owners, [[came[at] for at in came if at[1] == step] for step in range(n)]


def after(value, earlier):
    if earlier is not None:
        value, _ = lax.optimization_barrier((value, earlier))
    return value


def exchange(part, axis, mask, beside=None):
    came = lax.ppermute(part, axis, [(i, i ^ mask) for i in range(lax.axis_size(axis))])
    work = beside.pop(0) if beside else None
    return after(came, work() if callable(work) else work)


def row_sum(part, axis, beside=None):
    here = lax.axis_index(axis)
    others = lax.axis_size(axis) // 2
    half = part.shape[-2] // 2
    odd, place = here % 2, here // 2
    kept = lax.dynamic_slice_in_dim(part, odd * half, half, axis=-2)
    sent = lax.dynamic_slice_in_dim(part, (1 - odd) * half, half, axis=-2)
    part = kept + exchange(sent, axis, 1, beside)
    piece = half // others

    def piece_of(which):
        return lax.dynamic_slice_in_dim(part, which * piece, piece, axis=-2)

    came = [exchange(piece_of(place ^ d), axis, 2 * d) for d in range(1, others)]
    work = beside.pop(0) if beside else None
    came = after(came, work() if callable(work) else work)
    return functools.reduce(jnp.add, came, piece_of(place))


def row_gather(part, axis, beside=None):
    here = lax.axis_index(axis)
    others = lax.axis_size(axis) // 2
    odd, place = here % 2, here // 2
    pieces = [part] + [exchange(part, axis, 2 * d) for d in range(1, others)]
    work = beside.pop(0) if beside else None
    pieces = after(pieces, work() if callable(work) else work)
    bit = 1
    while bit < others:
        pieces = [
            jnp.where((place // bit) % 2 == 1, pieces[i ^ bit], pieces[i]) for i in range(others)
        ]
        bit *= 2
    part = jnp.concatenate(pieces, axis=-2)
    came = exchange(part, axis, 1, beside)
    return jnp.where(
        odd == 1,
        jnp.concatenate([came, part], axis=-2),
        jnp.concatenate([part, came], axis=-2),
    )


def response_codes(logratio, token_session, token_position, pad_mask):
    live = pad_mask.astype(jnp.float32)
    response = (token_session * LIST + token_position).astype(jnp.float32)
    return jnp.stack([live * logratio, jnp.where(pad_mask != 0, response, -1.0)])


def coefficients(codes):
    n, _, rows = codes.shape
    onehot = (
        codes[:, 1, :, None] == jnp.arange(SESSIONS * LIST, dtype=jnp.float32)
    ).astype(jnp.float32)
    sums = jnp.sum(onehot * codes[:, 0, :, None], axis=(0, 1))
    scores = math.sqrt(SESSIONS * LIST / (n * rows)) * sums
    response_grad = listwise_grad(scores)
    return 0.1 * jnp.sum(onehot * response_grad, axis=2)


def on_device(
    tokens,
    out_grad,
    logratio,
    token_session,
    token_position,
    pad_mask,
    w_in,
    m_in,
    v_in,
    w_out,
    m_out,
    v_out,
):
    n = lax.axis_size("col")
    here = lax.axis_index("col")
    codes = response_codes(logratio, token_session, token_position, pad_mask)
    codes = jnp.stack(
        [codes]
        + [
            lax.ppermute(codes, "col", [(i, (i + shift) % n) for i in range(n)])
            for shift in range(1, n)
        ]
    )
    out_grad, codes = lax.optimization_barrier((out_grad, codes))
    coeff = coefficients(codes)
    w_in16, w_out16 = lax.optimization_barrier(
        (w_in.astype(jnp.bfloat16), w_out.astype(jnp.bfloat16))
    )

    def scaled(shard, owner, earlier=None):
        mine = lax.dynamic_index_in_dim(coeff, (here - owner + n) % n, 0, keepdims=False)
        mine = after(mine, earlier)
        return (mine[:, None] * shard.astype(jnp.float32)).astype(jnp.bfloat16)

    def pre_of(shard):
        return jnp.dot(shard, w_in16, preferred_element_type=jnp.float32)

    def square(pre):
        positive = jnp.maximum(pre, 0.0)
        return (positive * positive).astype(jnp.bfloat16)

    def chain(pre, back):
        return (back * 2.0 * jnp.maximum(pre, 0.0)).astype(jnp.bfloat16)

    token_slots, owners, tokens_came = line_gather(tokens, "col")
    out_grad_slots, _, out_grads_came = line_gather(out_grad, "col")
    parts = next(p for p in (2, 3, 1) if w_out.shape[1] % (128 * p) == 0)
    outs_out = ()

    def update_part(part):
        def run():
            nonlocal outs_out
            outs_out = update(
                acts[-2:], dys[-2:], grad_out, w_out, m_out, v_out, 128, part, parts, outs_out
            )
            return outs_out

        return run

    dys = [scaled(out_grad, here)]
    pre = row_sum(pre_of(tokens), "row")
    acts, dpres = [row_gather(square(pre), "row")], []
    both = jnp.stack([against(dys[0], w_out16), pre_of(token_slots[1])])
    both = row_sum(after(both, (acts[0], tokens_came[1])), "row")
    both, pre = jnp.stack([chain(pre, both[0]), square(both[1])]), both[1]
    last = both = row_gather(both, "row")
    acts.append(both[1])
    dpres.append(both[0])
    for slot in range(1, n):
        if slot > 1:
            last = (last, tokens_came[slot])
            beside, latest = None, None
            if slot == n - 2:
                grad_in = grad_sum(token_slots[:slot], dpres, 256)
                grad_out = grad_sum(acts, dys, 128)
                beside = [None, (grad_in, grad_out)]
            if slot == n - 1:
                latest = [out_grads_came[slot]]
            pre = row_sum(after(pre_of(token_slots[slot]), last), "row", beside)
            last = row_gather(square(pre), "row", latest)
            acts.append(last)
        if slot < n - 1:
            dys.append(scaled(out_grad_slots[slot], owners[slot]))
            back = after(against(dys[slot], w_out16), (last, out_grads_came[slot]))
            last = row_gather(chain(pre, row_sum(back, "row")), "row")
            dpres.append(last)

    dys.append(scaled(out_grad_slots[n - 1], owners[n - 1], acts[-1]))
    work = [None] + [update_part(part) for part in range(parts)]
    back = row_sum(against(dys[n - 1], w_out16), "row", work)
    dpres.append(row_gather(chain(pre, back), "row", work))
    while work:
        work.pop(0)()
    outs_in = update(token_slots[-2:], dpres[-2:], grad_in, w_in, m_in, v_in, 256)
    return (*outs_in, *outs_out)


def solution(mesh):
    in_specs = (
        P("col", "row"),
        P("col", "row"),
        P("col"),
        P("col"),
        P("col"),
        P("col"),
        P("row", "col"),
        P("row", "col"),
        P("row", "col"),
        P("col", "row"),
        P("col", "row"),
        P("col", "row"),
    )
    out_specs = (
        P("row", "col"),
        P("row", "col"),
        P("row", "col"),
        P("col", "row"),
        P("col", "row"),
        P("col", "row"),
    )
    return jax.shard_map(
        on_device, mesh=mesh, in_specs=in_specs, out_specs=out_specs, check_vma=False
    )
```

```python
import functools
import math

import jax
import jax.numpy as jnp
from jax import lax
from jax.experimental import pallas as pl
from jax.experimental.pallas import tpu as pltpu
from jax.sharding import PartitionSpec as P

SESSIONS = 8
LIST = 4


def listwise_grad(scores):
    s = scores.reshape(SESSIONS, LIST)
    later = s[:, None, :] - s[:, :, None]
    order = jnp.arange(LIST)
    after = (order[None, :] > order[:, None]).astype(jnp.float32)
    before = (order[None, :] < order[:, None]).astype(jnp.float32)
    worse = -jnp.sum(after[None] * jax.nn.sigmoid(later), axis=2)
    better = jnp.sum(before[None] * jax.nn.sigmoid(-later), axis=2)
    return (worse + better).reshape(SESSIONS * LIST)


def adamw(weight, first, second, grad):
    new_first = 0.9 * first + 0.1 * grad
    new_second = 0.95 * second + 0.05 * (grad * grad)
    scaled = new_second * (1.0 / (1.0 - 0.95**20))
    below = scaled * lax.rsqrt(scaled) + 1e-08
    inverse = pl.reciprocal(below, approx=True)
    inverse = inverse * (2.0 - below * inverse)
    step = (0.0003 / (1.0 - 0.9**20)) * (new_first * inverse)
    return (weight * (1.0 - 0.0003 * 0.1) - step, new_first, new_second)


def over_rows(left, right):
    return lax.dot_general(
        left, right, (((0,), (0,)), ((), ())), preferred_element_type=jnp.float32
    )


def against(left, right):
    return lax.dot_general(
        left, right, (((1,), (1,)), ((), ())), preferred_element_type=jnp.float32
    )


def block_of(size, most):
    block = most
    while size % block:
        block -= 128
    return block


def fetch_kernel(parts, *refs):
    count = (len(refs) - 1) // (parts + 1)
    sources, targets, sems = refs[:count], refs[count:-1], refs[-1]
    copies = []
    for i, target in enumerate(targets):
        part, source = divmod(i, len(sources))
        width = target.shape[1]
        columns = sources[source].at[:, pl.ds(part * width, width)]
        copies.append(pltpu.make_async_copy(columns, target, sems.at[i]))
    for copy in copies:
        copy.start()
    for copy in copies:
        copy.wait()


def fetch(arrays, parts):
    shapes = [pltpu.VMEM((x.shape[0], x.shape[1] // parts), x.dtype) for x in arrays] * parts
    fetched = pl.pallas_call(
        functools.partial(fetch_kernel, parts),
        in_specs=[pl.BlockSpec(memory_space=pl.ANY)] * len(arrays),
        out_specs=[pl.BlockSpec(memory_space=pltpu.VMEM)] * len(shapes),
        out_shape=shapes,
        scratch_shapes=[pltpu.SemaphoreType.DMA((len(shapes),))],
        compiler_params=pltpu.CompilerParams(vmem_limit_bytes=26 * 2**20),
        cost_estimate=pl.CostEstimate(
            flops=0, bytes_accessed=4 * sum(x.size for x in arrays), transcendentals=0
        ),
    )(*arrays)
    return [fetched[i : i + len(arrays)] for i in range(0, len(shapes), len(arrays))]


def grad_kernel(pieces, *refs):
    lefts, rights, out = refs[:pieces], refs[pieces : 2 * pieces], refs[-1]
    total = refs[2 * pieces][...] if len(refs) > 2 * pieces + 1 else 0.0
    for left, right in zip(lefts, rights):
        total += over_rows(left[...], right[...])
    out[...] = total


def grad_sum(lefts, rights, most, so_far=()):
    rows, height = lefts[0].shape
    width = rights[0].shape[1]
    pieces = len(lefts)
    block = block_of(height, most)
    panel = pl.BlockSpec((block, width), lambda i: (i, 0))
    return pl.pallas_call(
        functools.partial(grad_kernel, pieces),
        grid=(height // block,),
        in_specs=[pl.BlockSpec((rows, block), lambda i: (0, i))] * pieces
        + [pl.BlockSpec((rows, width), lambda i: (0, 0))] * pieces
        + [panel] * len(so_far),
        out_specs=panel,
        out_shape=pltpu.VMEM((height, width), jnp.float32),
        input_output_aliases={2 * pieces + i: i for i in range(len(so_far))},
        compiler_params=pltpu.CompilerParams(vmem_limit_bytes=20 * 2**20),
        cost_estimate=pl.CostEstimate(
            flops=2 * pieces * rows * height * width,
            bytes_accessed=4 * height * width + 2 * pieces * rows * (height + width),
            transcendentals=0,
        ),
    )(*lefts, *rights, *so_far)


def update_kernel(left, right, grad, w, m, v, *refs):
    new_w, new_m, new_v = refs[-3:]
    total = grad[...] + over_rows(left[...], right[...])
    new_w[...], new_m[...], new_v[...] = adamw(w[...], m[...], v[...], total)


def update(left, right, grad, w, m, v, most, limit, part=0, parts=1, so_far=()):
    rows, height = left.shape
    width = right.shape[1] // parts
    block = block_of(height, most)
    panel = pl.BlockSpec((block, width), lambda i: (i, part))
    own = pl.BlockSpec((block, width), lambda i: (i, 0))
    shape = jax.ShapeDtypeStruct((height, right.shape[1]), jnp.float32)
    return pl.pallas_call(
        update_kernel,
        grid=(height // block,),
        in_specs=[
            pl.BlockSpec((rows, block), lambda i: (0, i)),
            pl.BlockSpec((rows, width), lambda i: (0, part)),
            panel,
        ]
        + [own] * 3
        + [pl.BlockSpec(memory_space=pl.ANY)] * len(so_far),
        out_specs=[panel] * 3,
        out_shape=[shape] * 3,
        input_output_aliases={6 + i: i for i in range(len(so_far))},
        compiler_params=pltpu.CompilerParams(vmem_limit_bytes=limit * 2**20),
        cost_estimate=pl.CostEstimate(
            flops=2 * rows * height * width,
            bytes_accessed=7 * 4 * height * width + 2 * rows * (height + width),
            transcendentals=2 * height * width,
        ),
    )(left, right, grad, w, m, v, *so_far)


def link_pairs(n, first, step):
    pairs = []
    for low in range(first, n - 1, 2):
        if low - (step - 1) >= 0:
            pairs.append((low, low + 1))
        if low + step <= n - 1:
            pairs.append((low + 1, low))
    return pairs


def arrivals(n, c):
    order = []
    for step in range(1, n):
        from_right, from_left = c + step <= n - 1, c - step >= 0
        over = (from_right, from_left) if c % 2 == 0 else (from_left, from_right)
        order += [(links, step) for links in (0, 1) if over[links]]
    return order


def line_gather(shard, axis):
    n = lax.axis_size(axis)
    here = lax.axis_index(axis)
    came = {(0, 0): shard, (1, 0): shard}
    for step in range(1, n):
        arrived = {}
        for links in (0, 1):
            pairs = link_pairs(n, links, step)
            if pairs:
                arrived[links, step] = lax.ppermute(came[1 - links, step - 1], axis, pairs)
        came.update(lax.optimization_barrier(arrived))
    slots, owners = [shard], [here]
    tables = [arrivals(n, c) for c in range(n)]
    for slot in range(n - 1):
        users = {}
        origins = []
        for c in range(n):
            links, step = tables[c][slot]
            users.setdefault((links, step), []).append(c)
            origins.append(c + step if links == c % 2 else c - step)
        choice = None
        for source, places in users.items():
            if choice is None:
                choice = came[source]
            else:
                mine = functools.reduce(jnp.logical_or, [here == c for c in places])
                choice = jnp.where(mine, came[source], choice)
        slots.append(choice)
        owners.append(jnp.array(origins, dtype=jnp.int32)[here])
    return slots, owners, [[came[at] for at in came if at[1] == step] for step in range(n)]


def after(value, earlier):
    if earlier is not None:
        value, _ = lax.optimization_barrier((value, earlier))
    return value


def exchange(part, axis, mask, beside=None):
    came = lax.ppermute(part, axis, [(i, i ^ mask) for i in range(lax.axis_size(axis))])
    work = beside.pop(0) if beside else None
    return after(came, work() if callable(work) else work)


def row_sum(part, axis, beside=None):
    here = lax.axis_index(axis)
    others = lax.axis_size(axis) // 2
    half = part.shape[-2] // 2
    odd, place = here % 2, here // 2
    kept = lax.dynamic_slice_in_dim(part, odd * half, half, axis=-2)
    sent = lax.dynamic_slice_in_dim(part, (1 - odd) * half, half, axis=-2)
    part = kept + exchange(sent, axis, 1, beside)
    piece = half // others

    def piece_of(which):
        return lax.dynamic_slice_in_dim(part, which * piece, piece, axis=-2)

    came = [exchange(piece_of(place ^ d), axis, 2 * d) for d in range(1, others)]
    work = beside.pop(0) if beside else None
    came = after(came, work() if callable(work) else work)
    return functools.reduce(jnp.add, came, piece_of(place))


def row_gather(part, axis, beside=None):
    here = lax.axis_index(axis)
    others = lax.axis_size(axis) // 2
    odd, place = here % 2, here // 2
    pieces = [part] + [exchange(part, axis, 2 * d) for d in range(1, others)]
    work = beside.pop(0) if beside else None
    pieces = after(pieces, work() if callable(work) else work)
    bit = 1
    while bit < others:
        pieces = [
            jnp.where((place // bit) % 2 == 1, pieces[i ^ bit], pieces[i]) for i in range(others)
        ]
        bit *= 2
    part = jnp.concatenate(pieces, axis=-2)
    came = exchange(part, axis, 1, beside)
    return jnp.where(
        odd == 1,
        jnp.concatenate([came, part], axis=-2),
        jnp.concatenate([part, came], axis=-2),
    )


def response_codes(logratio, token_session, token_position, pad_mask):
    live = pad_mask.astype(jnp.float32)
    response = (token_session * LIST + token_position).astype(jnp.float32)
    return jnp.stack([live * logratio, jnp.where(pad_mask != 0, response, -1.0)])


def coefficients(codes):
    n, _, rows = codes.shape
    onehot = (
        codes[:, 1, :, None] == jnp.arange(SESSIONS * LIST, dtype=jnp.float32)
    ).astype(jnp.float32)
    sums = jnp.sum(onehot * codes[:, 0, :, None], axis=(0, 1))
    scores = math.sqrt(SESSIONS * LIST / (n * rows)) * sums
    response_grad = listwise_grad(scores)
    return 0.1 * jnp.sum(onehot * response_grad, axis=2)


def on_device(
    tokens,
    out_grad,
    logratio,
    token_session,
    token_position,
    pad_mask,
    w_in,
    m_in,
    v_in,
    w_out,
    m_out,
    v_out,
):
    n = lax.axis_size("col")
    here = lax.axis_index("col")
    codes = response_codes(logratio, token_session, token_position, pad_mask)
    codes = jnp.stack(
        [codes]
        + [
            lax.ppermute(codes, "col", [(i, (i + shift) % n) for i in range(n)])
            for shift in range(1, n)
        ]
    )
    out_grad, codes = lax.optimization_barrier((out_grad, codes))
    coeff = coefficients(codes)
    w_in16, w_out16 = lax.optimization_barrier(
        (w_in.astype(jnp.bfloat16), w_out.astype(jnp.bfloat16))
    )

    def scaled(shard, owner, earlier=None):
        mine = lax.dynamic_index_in_dim(coeff, (here - owner + n) % n, 0, keepdims=False)
        mine = after(mine, earlier)
        return (mine[:, None] * shard.astype(jnp.float32)).astype(jnp.bfloat16)

    def pre_of(shard):
        return jnp.dot(shard, w_in16, preferred_element_type=jnp.float32)

    def square(pre):
        positive = jnp.maximum(pre, 0.0)
        return (positive * positive).astype(jnp.bfloat16)

    def chain(pre, back):
        return (back * 2.0 * jnp.maximum(pre, 0.0)).astype(jnp.bfloat16)

    token_slots, owners, tokens_came = line_gather(tokens, "col")
    out_grad_slots, _, out_grads_came = line_gather(out_grad, "col")
    parts = next(p for p in (2, 3, 1) if w_out.shape[1] % (128 * p) == 0)
    outs_out = ()

    def update_part(part):
        def run():
            nonlocal outs_out
            outs_out = update(
                acts[-1], dys[-1], grad_out, *state_out[part], 128, 20, part, parts, outs_out
            )
            return outs_out

        return run

    dys = [scaled(out_grad, here)]
    pre = row_sum(pre_of(tokens), "row")
    acts, dpres = [row_gather(square(pre), "row")], []
    both = jnp.stack([against(dys[0], w_out16), pre_of(token_slots[1])])
    both = row_sum(after(both, (acts[0], tokens_came[1])), "row")
    both, pre = jnp.stack([chain(pre, both[0]), square(both[1])]), both[1]
    last = both = row_gather(both, "row")
    acts.append(both[1])
    dpres.append(both[0])
    for slot in range(1, n):
        if slot > 1:
            last = (last, tokens_came[slot])
            beside, latest = None, None
            if slot == n - 2:
                grad_in = grad_sum(token_slots[:slot], dpres, 256)
                grad_out = grad_sum(acts, dys, 128)
                state_out = fetch((w_out, m_out, v_out), parts)
                beside = [None, (grad_in, grad_out, state_out)]
            if slot == n - 1:
                grad_in = grad_sum(token_slots[slot - 1 : slot], dpres[-1:], 256, (grad_in,))
                grad_out = grad_sum(acts[-1:], dys[-1:], 128, (grad_out,))
                beside, latest = [None, (grad_in, grad_out)], [out_grads_came[slot]]
            pre = row_sum(after(pre_of(token_slots[slot]), last), "row", beside)
            last = row_gather(square(pre), "row", latest)
            acts.append(last)
        if slot < n - 1:
            dys.append(scaled(out_grad_slots[slot], owners[slot]))
            back = after(against(dys[slot], w_out16), (last, out_grads_came[slot]))
            last = row_gather(chain(pre, row_sum(back, "row")), "row")
            dpres.append(last)

    dys.append(scaled(out_grad_slots[n - 1], owners[n - 1], acts[-1]))
    work = [None] + [update_part(part) for part in range(parts)]
    back = row_sum(against(dys[n - 1], w_out16), "row", work)
    dpres.append(row_gather(chain(pre, back), "row", work))
    while work:
        work.pop(0)()
    outs_in = update(token_slots[-1], dpres[-1], grad_in, w_in, m_in, v_in, 256, 42)
    return (*outs_in, *outs_out)


def solution(mesh):
    in_specs = (
        P("col", "row"),
        P("col", "row"),
        P("col"),
        P("col"),
        P("col"),
        P("col"),
        P("row", "col"),
        P("row", "col"),
        P("row", "col"),
        P("col", "row"),
        P("col", "row"),
        P("col", "row"),
    )
    out_specs = (
        P("row", "col"),
        P("row", "col"),
        P("row", "col"),
        P("col", "row"),
        P("col", "row"),
        P("col", "row"),
    )
    return jax.shard_map(
        on_device, mesh=mesh, in_specs=in_specs, out_specs=out_specs, check_vma=False
    )
```

```python
import functools
import math

import jax
import jax.numpy as jnp
from jax import lax
from jax.experimental import pallas as pl
from jax.experimental.pallas import tpu as pltpu
from jax.sharding import PartitionSpec as P

SESSIONS = 8
LIST = 4


def listwise_grad(scores):
    s = scores.reshape(SESSIONS, LIST)
    later = s[:, None, :] - s[:, :, None]
    order = jnp.arange(LIST)
    after = (order[None, :] > order[:, None]).astype(jnp.float32)
    before = (order[None, :] < order[:, None]).astype(jnp.float32)
    worse = -jnp.sum(after[None] * jax.nn.sigmoid(later), axis=2)
    better = jnp.sum(before[None] * jax.nn.sigmoid(-later), axis=2)
    return (worse + better).reshape(SESSIONS * LIST)


def adamw(weight, first, second, grad):
    new_first = 0.9 * first + 0.1 * grad
    new_second = 0.95 * second + 0.05 * (grad * grad)
    scaled = new_second * (1.0 / (1.0 - 0.95**20))
    below = scaled * lax.rsqrt(scaled) + 1e-08
    inverse = pl.reciprocal(below, approx=True)
    inverse = inverse * (2.0 - below * inverse)
    step = (0.0003 / (1.0 - 0.9**20)) * (new_first * inverse)
    return (weight * (1.0 - 0.0003 * 0.1) - step, new_first, new_second)


def over_rows(left, right):
    return lax.dot_general(
        left, right, (((0,), (0,)), ((), ())), preferred_element_type=jnp.float32
    )


def against(left, right):
    return lax.dot_general(
        left, right, (((1,), (1,)), ((), ())), preferred_element_type=jnp.float32
    )


def block_of(size, most):
    block = most
    while size % block:
        block -= 128
    return block


def fetch_kernel(count, axis, part, *refs):
    sources, targets, sems = refs[:count], refs[-1 - count : -1], refs[-1]
    copies = []
    for i, (source, target) in enumerate(zip(sources, targets)):
        size = target.shape[axis]
        span = pl.ds(part * size, size)
        source = source.at[span, :] if axis == 0 else source.at[:, span]
        copies.append(pltpu.make_async_copy(source, target, sems.at[i]))
    for copy in copies:
        copy.start()
    for copy in copies:
        copy.wait()


def fetch(arrays, axis, part, parts, earlier=()):
    shape = list(arrays[0].shape)
    shape[axis] //= parts
    count = len(arrays)
    return pl.pallas_call(
        functools.partial(fetch_kernel, count, axis, part),
        in_specs=[pl.BlockSpec(memory_space=pltpu.HBM)] * (count + len(earlier)),
        out_specs=[pl.BlockSpec(memory_space=pltpu.VMEM)] * count,
        out_shape=[pltpu.VMEM(tuple(shape), jnp.float32)] * count,
        scratch_shapes=[pltpu.SemaphoreType.DMA((count,))],
        compiler_params=pltpu.CompilerParams(vmem_limit_bytes=4 * 2**20),
        cost_estimate=pl.CostEstimate(
            flops=0, bytes_accessed=4 * count * math.prod(shape), transcendentals=0
        ),
    )(*[pltpu.with_memory_space_constraint(x, pltpu.HBM) for x in (*arrays, *earlier)])


def grad_kernel(pieces, *refs):
    lefts, rights, out = refs[:pieces], refs[pieces : 2 * pieces], refs[-1]
    total = refs[2 * pieces][...] if len(refs) > 2 * pieces + 1 else 0.0
    for left, right in zip(lefts, rights):
        total += over_rows(left[...], right[...])
    out[...] = total


def grad_sum(lefts, rights, most, so_far=()):
    rows, height = lefts[0].shape
    width = rights[0].shape[1]
    pieces = len(lefts)
    block = block_of(height, most)
    panel = pl.BlockSpec((block, width), lambda i: (i, 0))
    return pl.pallas_call(
        functools.partial(grad_kernel, pieces),
        grid=(height // block,),
        in_specs=[pl.BlockSpec((rows, block), lambda i: (0, i))] * pieces
        + [pl.BlockSpec((rows, width), lambda i: (0, 0))] * pieces
        + [panel] * len(so_far),
        out_specs=panel,
        out_shape=pltpu.VMEM((height, width), jnp.float32),
        input_output_aliases={2 * pieces + i: i for i in range(len(so_far))},
        compiler_params=pltpu.CompilerParams(vmem_limit_bytes=16 * 2**20),
        cost_estimate=pl.CostEstimate(
            flops=2 * pieces * rows * height * width,
            bytes_accessed=4 * height * width + 2 * pieces * rows * (height + width),
            transcendentals=0,
        ),
    )(*lefts, *rights, *so_far)


def update_kernel(left, right, grad, w, m, v, *refs):
    new_w, new_m, new_v = refs[-3:]
    total = grad[...] + over_rows(left[...], right[...])
    new_w[...], new_m[...], new_v[...] = adamw(w[...], m[...], v[...], total)


def update(left, right, grad, state, most, axis, part, parts, so_far=()):
    rows = left.shape[0]
    height, width = state[0].shape
    block = block_of(height, most)
    steps = height // block
    row0, column = (part * steps, 0) if axis == 0 else (0, part)
    panel = pl.BlockSpec((block, width), lambda i: (row0 + i, column))
    own = pl.BlockSpec((block, width), lambda i: (i, 0))
    shape = jax.ShapeDtypeStruct((left.shape[1], right.shape[1]), jnp.float32)
    return pl.pallas_call(
        update_kernel,
        grid=(steps,),
        in_specs=[
            pl.BlockSpec((rows, block), lambda i: (0, row0 + i)),
            pl.BlockSpec((rows, width), lambda i: (0, column)),
            panel,
        ]
        + [own] * 3
        + [pl.BlockSpec(memory_space=pl.ANY)] * len(so_far),
        out_specs=[panel] * 3,
        out_shape=[shape] * 3,
        input_output_aliases={6 + i: i for i in range(len(so_far))},
        compiler_params=pltpu.CompilerParams(vmem_limit_bytes=16 * 2**20),
        cost_estimate=pl.CostEstimate(
            flops=2 * rows * height * width,
            bytes_accessed=7 * 4 * height * width + 2 * rows * (height + width),
            transcendentals=2 * height * width,
        ),
    )(left, right, grad, *state, *so_far)


def link_pairs(n, first, step):
    pairs = []
    for low in range(first, n - 1, 2):
        if low - (step - 1) >= 0:
            pairs.append((low, low + 1))
        if low + step <= n - 1:
            pairs.append((low + 1, low))
    return pairs


def arrivals(n, c):
    order = []
    for step in range(1, n):
        from_right, from_left = c + step <= n - 1, c - step >= 0
        over = (from_right, from_left) if c % 2 == 0 else (from_left, from_right)
        order += [(links, step) for links in (0, 1) if over[links]]
    return order


def line_gather(shard, axis):
    n = lax.axis_size(axis)
    here = lax.axis_index(axis)
    came = {(0, 0): shard, (1, 0): shard}
    for step in range(1, n):
        arrived = {}
        for links in (0, 1):
            pairs = link_pairs(n, links, step)
            if pairs:
                arrived[links, step] = lax.ppermute(came[1 - links, step - 1], axis, pairs)
        came.update(lax.optimization_barrier(arrived))
    slots, owners = [shard], [here]
    tables = [arrivals(n, c) for c in range(n)]
    for slot in range(n - 1):
        users = {}
        origins = []
        for c in range(n):
            links, step = tables[c][slot]
            users.setdefault((links, step), []).append(c)
            origins.append(c + step if links == c % 2 else c - step)
        choice = None
        for source, places in users.items():
            if choice is None:
                choice = came[source]
            else:
                mine = functools.reduce(jnp.logical_or, [here == c for c in places])
                choice = jnp.where(mine, came[source], choice)
        slots.append(choice)
        owners.append(jnp.array(origins, dtype=jnp.int32)[here])
    return slots, owners, [[came[at] for at in came if at[1] == step] for step in range(n)]


def after(value, earlier):
    if earlier is not None:
        value, _ = lax.optimization_barrier((value, earlier))
    return value


def exchange(part, axis, mask, beside=None):
    came = lax.ppermute(part, axis, [(i, i ^ mask) for i in range(lax.axis_size(axis))])
    work = beside.pop(0) if beside else None
    return after(came, work() if callable(work) else work)


def row_sum(part, axis, beside=None):
    here = lax.axis_index(axis)
    others = lax.axis_size(axis) // 2
    half = part.shape[-2] // 2
    odd, place = here % 2, here // 2
    kept = lax.dynamic_slice_in_dim(part, odd * half, half, axis=-2)
    sent = lax.dynamic_slice_in_dim(part, (1 - odd) * half, half, axis=-2)
    part = kept + exchange(sent, axis, 1, beside)
    piece = half // others

    def piece_of(which):
        return lax.dynamic_slice_in_dim(part, which * piece, piece, axis=-2)

    came = [exchange(piece_of(place ^ d), axis, 2 * d) for d in range(1, others)]
    work = beside.pop(0) if beside else None
    came = after(came, work() if callable(work) else work)
    return functools.reduce(jnp.add, came, piece_of(place))


def row_gather(part, axis, beside=None):
    here = lax.axis_index(axis)
    others = lax.axis_size(axis) // 2
    odd, place = here % 2, here // 2
    pieces = [part] + [exchange(part, axis, 2 * d) for d in range(1, others)]
    work = beside.pop(0) if beside else None
    pieces = after(pieces, work() if callable(work) else work)
    bit = 1
    while bit < others:
        pieces = [
            jnp.where((place // bit) % 2 == 1, pieces[i ^ bit], pieces[i]) for i in range(others)
        ]
        bit *= 2
    part = jnp.concatenate(pieces, axis=-2)
    came = exchange(part, axis, 1, beside)
    return jnp.where(
        odd == 1,
        jnp.concatenate([came, part], axis=-2),
        jnp.concatenate([part, came], axis=-2),
    )


def response_codes(logratio, token_session, token_position, pad_mask):
    live = pad_mask.astype(jnp.float32)
    response = (token_session * LIST + token_position).astype(jnp.float32)
    return jnp.stack([live * logratio, jnp.where(pad_mask != 0, response, -1.0)])


def coefficients(codes):
    n, _, rows = codes.shape
    onehot = (
        codes[:, 1, :, None] == jnp.arange(SESSIONS * LIST, dtype=jnp.float32)
    ).astype(jnp.float32)
    sums = jnp.sum(onehot * codes[:, 0, :, None], axis=(0, 1))
    scores = math.sqrt(SESSIONS * LIST / (n * rows)) * sums
    response_grad = listwise_grad(scores)
    return 0.1 * jnp.sum(onehot * response_grad, axis=2)


def on_device(
    tokens,
    out_grad,
    logratio,
    token_session,
    token_position,
    pad_mask,
    w_in,
    m_in,
    v_in,
    w_out,
    m_out,
    v_out,
):
    n = lax.axis_size("col")
    here = lax.axis_index("col")
    codes = response_codes(logratio, token_session, token_position, pad_mask)
    codes = jnp.stack(
        [codes]
        + [
            lax.ppermute(codes, "col", [(i, (i + shift) % n) for i in range(n)])
            for shift in range(1, n)
        ]
    )
    out_grad, codes = lax.optimization_barrier((out_grad, codes))
    coeff = coefficients(codes)
    w_in16, w_out16 = lax.optimization_barrier(
        (w_in.astype(jnp.bfloat16), w_out.astype(jnp.bfloat16))
    )

    def scaled(shard, owner, earlier=None):
        mine = lax.dynamic_index_in_dim(coeff, (here - owner + n) % n, 0, keepdims=False)
        mine = after(mine, earlier)
        return (mine[:, None] * shard.astype(jnp.float32)).astype(jnp.bfloat16)

    def pre_of(shard):
        return jnp.dot(shard, w_in16, preferred_element_type=jnp.float32)

    def square(pre):
        positive = jnp.maximum(pre, 0.0)
        return (positive * positive).astype(jnp.bfloat16)

    def chain(pre, back):
        return (back * 2.0 * jnp.maximum(pre, 0.0)).astype(jnp.bfloat16)

    token_slots, owners, tokens_came = line_gather(tokens, "col")
    out_grad_slots, _, out_grads_came = line_gather(out_grad, "col")
    parts = 2 if w_out.shape[1] % 256 == 0 else 1
    parts_in = 2 if w_in.shape[0] % 256 == 0 else 1
    dys = [scaled(out_grad, here)]
    pre = row_sum(pre_of(tokens), "row")
    acts, dpres = [row_gather(square(pre), "row")], []
    both = jnp.stack([against(dys[0], w_out16), pre_of(token_slots[1])])
    both = row_sum(after(both, (acts[0], tokens_came[1])), "row")
    both, pre = jnp.stack([chain(pre, both[0]), square(both[1])]), both[1]
    last = both = row_gather(both, "row")
    acts.append(both[1])
    dpres.append(both[0])
    for slot in range(1, n):
        if slot > 1:
            last = (last, tokens_came[slot])
            beside, latest = None, None
            if slot == n - 2:
                grad_in = grad_sum(token_slots[:slot], dpres, 256)
                grad_out = grad_sum(acts, dys, 128)
                states_out = [fetch((w_out, m_out, v_out), 1, p, parts) for p in range(parts)]
                beside = [None, (grad_in, grad_out, states_out)]
            if slot == n - 1:
                grad_in = grad_sum(token_slots[slot - 1 : slot], dpres[-1:], 256, (grad_in,))
                grad_out = grad_sum(acts[-1:], dys[-1:], 128, (grad_out,))
                beside, latest = [None, (grad_in, grad_out)], [out_grads_came[slot]]
            pre = row_sum(after(pre_of(token_slots[slot]), last), "row", beside)
            last = row_gather(square(pre), "row", latest)
            acts.append(last)
        if slot < n - 1:
            dys.append(scaled(out_grad_slots[slot], owners[slot]))
            back = after(against(dys[slot], w_out16), (last, out_grads_came[slot]))
            last = row_gather(chain(pre, row_sum(back, "row")), "row")
            dpres.append(last)

    dys.append(scaled(out_grad_slots[n - 1], owners[n - 1], acts[-1]))
    outs_out, states_in = (), []

    def update_out(part):
        nonlocal outs_out
        outs_out = update(
            acts[-1], dys[-1], grad_out, states_out[part], 128, 1, part, parts, outs_out
        )
        return outs_out

    def state_in(part):
        states_in.append(fetch((w_in, m_in, v_in), 0, part, parts_in, outs_out))
        return states_in[part]

    runs = [lambda p=p: update_out(p) for p in range(parts)]
    for p in range(parts_in):
        runs.insert(1 + 2 * p, lambda p=p: state_in(p))
    work = [None, runs[0], lambda: [run() for run in runs[1:-1]], runs[-1]]
    back = row_sum(against(dys[n - 1], w_out16), "row", work)
    dpres.append(row_gather(chain(pre, back), "row", work))
    outs_in = ()
    for p in range(parts_in):
        outs_in = update(
            token_slots[-1], dpres[-1], grad_in, states_in[p], 256, 0, p, parts_in, outs_in
        )
    return (*outs_in, *outs_out)


def solution(mesh):
    in_specs = (
        P("col", "row"),
        P("col", "row"),
        P("col"),
        P("col"),
        P("col"),
        P("col"),
        P("row", "col"),
        P("row", "col"),
        P("row", "col"),
        P("col", "row"),
        P("col", "row"),
        P("col", "row"),
    )
    out_specs = (
        P("row", "col"),
        P("row", "col"),
        P("row", "col"),
        P("col", "row"),
        P("col", "row"),
        P("col", "row"),
    )
    return jax.shard_map(
        on_device, mesh=mesh, in_specs=in_specs, out_specs=out_specs, check_vma=False
    )
```

```python
import functools
import math

import jax
import jax.numpy as jnp
from jax import lax
from jax.experimental import pallas as pl
from jax.experimental.pallas import tpu as pltpu
from jax.sharding import PartitionSpec as P

SESSIONS = 8
LIST = 4


def listwise_grad(scores):
    s = scores.reshape(SESSIONS, LIST)
    later = s[:, None, :] - s[:, :, None]
    order = jnp.arange(LIST)
    after = (order[None, :] > order[:, None]).astype(jnp.float32)
    before = (order[None, :] < order[:, None]).astype(jnp.float32)
    worse = -jnp.sum(after[None] * jax.nn.sigmoid(later), axis=2)
    better = jnp.sum(before[None] * jax.nn.sigmoid(-later), axis=2)
    return (worse + better).reshape(SESSIONS * LIST)


def adamw(weight, first, second, grad):
    new_first = 0.9 * first + 0.1 * grad
    new_second = 0.95 * second + 0.05 * (grad * grad)
    scaled = new_second * (1.0 / (1.0 - 0.95**20))
    below = scaled * lax.rsqrt(scaled) + 1e-08
    inverse = pl.reciprocal(below, approx=True)
    inverse = inverse * (2.0 - below * inverse)
    step = (0.0003 / (1.0 - 0.9**20)) * (new_first * inverse)
    return (weight * (1.0 - 0.0003 * 0.1) - step, new_first, new_second)


def over_rows(left, right):
    return lax.dot_general(
        left, right, (((0,), (0,)), ((), ())), preferred_element_type=jnp.float32
    )


def against(left, right):
    return lax.dot_general(
        left, right, (((1,), (1,)), ((), ())), preferred_element_type=jnp.float32
    )


def block_of(size, most):
    block = most
    while size % block:
        block -= 128
    return block


def fetch_kernel(parts, *refs):
    count = (len(refs) - 1) // (parts + 1)
    sources, targets, sems = refs[:count], refs[count:-1], refs[-1]
    copies = []
    for i, target in enumerate(targets):
        part, source = divmod(i, len(sources))
        width = target.shape[1]
        columns = sources[source].at[:, pl.ds(part * width, width)]
        copies.append(pltpu.make_async_copy(columns, target, sems.at[i]))
    for copy in copies:
        copy.start()
    for copy in copies:
        copy.wait()


def fetch(arrays, parts):
    shapes = [pltpu.VMEM((x.shape[0], x.shape[1] // parts), x.dtype) for x in arrays] * parts
    fetched = pl.pallas_call(
        functools.partial(fetch_kernel, parts),
        in_specs=[pl.BlockSpec(memory_space=pltpu.HBM)] * len(arrays),
        out_specs=[pl.BlockSpec(memory_space=pltpu.VMEM)] * len(shapes),
        out_shape=shapes,
        scratch_shapes=[pltpu.SemaphoreType.DMA((len(shapes),))],
        compiler_params=pltpu.CompilerParams(vmem_limit_bytes=4 * 2**20),
        cost_estimate=pl.CostEstimate(
            flops=0, bytes_accessed=4 * sum(x.size for x in arrays), transcendentals=0
        ),
    )(*[pltpu.with_memory_space_constraint(x, pltpu.HBM) for x in arrays])
    return [fetched[i : i + len(arrays)] for i in range(0, len(shapes), len(arrays))]


def grad_kernel(pieces, *refs):
    lefts, rights, out = refs[:pieces], refs[pieces : 2 * pieces], refs[-1]
    total = refs[2 * pieces][...] if len(refs) > 2 * pieces + 1 else 0.0
    for left, right in zip(lefts, rights):
        total += over_rows(left[...], right[...])
    out[...] = total


def grad_sum(lefts, rights, most, so_far=()):
    rows, height = lefts[0].shape
    width = rights[0].shape[1]
    pieces = len(lefts)
    block = block_of(height, most)
    panel = pl.BlockSpec((block, width), lambda i: (i, 0))
    return pl.pallas_call(
        functools.partial(grad_kernel, pieces),
        grid=(height // block,),
        in_specs=[pl.BlockSpec((rows, block), lambda i: (0, i))] * pieces
        + [pl.BlockSpec((rows, width), lambda i: (0, 0))] * pieces
        + [panel] * len(so_far),
        out_specs=panel,
        out_shape=pltpu.VMEM((height, width), jnp.float32),
        input_output_aliases={2 * pieces + i: i for i in range(len(so_far))},
        compiler_params=pltpu.CompilerParams(vmem_limit_bytes=16 * 2**20),
        cost_estimate=pl.CostEstimate(
            flops=2 * pieces * rows * height * width,
            bytes_accessed=4 * height * width + 2 * pieces * rows * (height + width),
            transcendentals=0,
        ),
    )(*lefts, *rights, *so_far)


def update_kernel(resident, part, left, right, grad, w, m, v, *refs):
    new_w, new_m, new_v, late = refs[-4:]
    block, width = late.shape
    count = 16 if width <= 768 else 8
    late[...] = over_rows(left[...], right[...])

    def some_rows(i, carry):
        rows = pl.ds(pl.multiple_of(count * i, count), count)
        far = pl.ds(pl.multiple_of(pl.program_id(0) * block + count * i, count), count)
        own = far if resident else rows
        total = grad[far, part * width : (part + 1) * width] + late[rows, :]
        new_w[rows, :], new_m[rows, :], new_v[rows, :] = adamw(
            w[own, :], m[own, :], v[own, :], total
        )
        return carry

    lax.fori_loop(0, block // count, some_rows, 0, unroll=4)


def update(left, right, grad, state, most, limit, resident, part=0, parts=1, so_far=()):
    rows, height = left.shape
    width = right.shape[1] // parts
    block = block_of(height, most)
    panel = pl.BlockSpec((block, width), lambda i: (i, part))
    whole = pl.BlockSpec(memory_space=pltpu.VMEM)
    own = whole if resident else pl.BlockSpec((block, width), lambda i: (i, 0))
    shape = jax.ShapeDtypeStruct((height, right.shape[1]), jnp.float32)
    if resident:
        state = [pltpu.with_memory_space_constraint(x, pltpu.VMEM) for x in state]
    return pl.pallas_call(
        functools.partial(update_kernel, resident, part),
        grid=(height // block,),
        in_specs=[
            pl.BlockSpec((rows, block), lambda i: (0, i)),
            pl.BlockSpec((rows, width), lambda i: (0, part)),
            whole,
        ]
        + [own] * 3
        + [pl.BlockSpec(memory_space=pl.ANY)] * len(so_far),
        out_specs=[panel] * 3,
        out_shape=[shape] * 3,
        scratch_shapes=[pltpu.VMEM((block, width), jnp.float32)],
        input_output_aliases={6 + i: i for i in range(len(so_far))},
        compiler_params=pltpu.CompilerParams(vmem_limit_bytes=limit * 2**20),
        cost_estimate=pl.CostEstimate(
            flops=2 * rows * height * width,
            bytes_accessed=7 * 4 * height * width + 2 * rows * (height + width),
            transcendentals=2 * height * width,
        ),
    )(left, right, pltpu.with_memory_space_constraint(grad, pltpu.VMEM), *state, *so_far)


def link_pairs(n, first, step):
    pairs = []
    for low in range(first, n - 1, 2):
        if low - (step - 1) >= 0:
            pairs.append((low, low + 1))
        if low + step <= n - 1:
            pairs.append((low + 1, low))
    return pairs


def arrivals(n, c):
    order = []
    for step in range(1, n):
        from_right, from_left = c + step <= n - 1, c - step >= 0
        over = (from_right, from_left) if c % 2 == 0 else (from_left, from_right)
        order += [(links, step) for links in (0, 1) if over[links]]
    return order


def line_gather(shard, axis):
    n = lax.axis_size(axis)
    here = lax.axis_index(axis)
    came = {(0, 0): shard, (1, 0): shard}
    for step in range(1, n):
        arrived = {}
        for links in (0, 1):
            pairs = link_pairs(n, links, step)
            if pairs:
                arrived[links, step] = lax.ppermute(came[1 - links, step - 1], axis, pairs)
        came.update(lax.optimization_barrier(arrived))
    slots, owners = [shard], [here]
    tables = [arrivals(n, c) for c in range(n)]
    for slot in range(n - 1):
        users = {}
        origins = []
        for c in range(n):
            links, step = tables[c][slot]
            users.setdefault((links, step), []).append(c)
            origins.append(c + step if links == c % 2 else c - step)
        choice = None
        for source, places in users.items():
            if choice is None:
                choice = came[source]
            else:
                mine = functools.reduce(jnp.logical_or, [here == c for c in places])
                choice = jnp.where(mine, came[source], choice)
        slots.append(choice)
        owners.append(jnp.array(origins, dtype=jnp.int32)[here])
    return slots, owners, [[came[at] for at in came if at[1] == step] for step in range(n)]


def after(value, earlier):
    if earlier is not None:
        value, _ = lax.optimization_barrier((value, earlier))
    return value


def exchange(part, axis, mask, beside=None):
    came = lax.ppermute(part, axis, [(i, i ^ mask) for i in range(lax.axis_size(axis))])
    work = beside.pop(0) if beside else None
    return after(came, work() if callable(work) else work)


def row_sum(part, axis, beside=None):
    here = lax.axis_index(axis)
    others = lax.axis_size(axis) // 2
    half = part.shape[-2] // 2
    odd, place = here % 2, here // 2
    kept = lax.dynamic_slice_in_dim(part, odd * half, half, axis=-2)
    sent = lax.dynamic_slice_in_dim(part, (1 - odd) * half, half, axis=-2)
    part = kept + exchange(sent, axis, 1, beside)
    piece = half // others

    def piece_of(which):
        return lax.dynamic_slice_in_dim(part, which * piece, piece, axis=-2)

    came = [exchange(piece_of(place ^ d), axis, 2 * d) for d in range(1, others)]
    work = beside.pop(0) if beside else None
    came = after(came, work() if callable(work) else work)
    return functools.reduce(jnp.add, came, piece_of(place))


def row_gather(part, axis, beside=None):
    here = lax.axis_index(axis)
    others = lax.axis_size(axis) // 2
    odd, place = here % 2, here // 2
    pieces = [part] + [exchange(part, axis, 2 * d) for d in range(1, others)]
    work = beside.pop(0) if beside else None
    pieces = after(pieces, work() if callable(work) else work)
    bit = 1
    while bit < others:
        pieces = [
            jnp.where((place // bit) % 2 == 1, pieces[i ^ bit], pieces[i]) for i in range(others)
        ]
        bit *= 2
    part = jnp.concatenate(pieces, axis=-2)
    came = exchange(part, axis, 1, beside)
    return jnp.where(
        odd == 1,
        jnp.concatenate([came, part], axis=-2),
        jnp.concatenate([part, came], axis=-2),
    )


def response_codes(logratio, token_session, token_position, pad_mask):
    live = pad_mask.astype(jnp.float32)
    response = (token_session * LIST + token_position).astype(jnp.float32)
    return jnp.stack([live * logratio, jnp.where(pad_mask != 0, response, -1.0)])


def coefficients(codes):
    n, _, rows = codes.shape
    onehot = (
        codes[:, 1, :, None] == jnp.arange(SESSIONS * LIST, dtype=jnp.float32)
    ).astype(jnp.float32)
    sums = jnp.sum(onehot * codes[:, 0, :, None], axis=(0, 1))
    scores = math.sqrt(SESSIONS * LIST / (n * rows)) * sums
    response_grad = listwise_grad(scores)
    return 0.1 * jnp.sum(onehot * response_grad, axis=2)


def on_device(
    tokens,
    out_grad,
    logratio,
    token_session,
    token_position,
    pad_mask,
    w_in,
    m_in,
    v_in,
    w_out,
    m_out,
    v_out,
):
    n = lax.axis_size("col")
    here = lax.axis_index("col")
    codes = response_codes(logratio, token_session, token_position, pad_mask)
    codes = jnp.stack(
        [codes]
        + [
            lax.ppermute(codes, "col", [(i, (i + shift) % n) for i in range(n)])
            for shift in range(1, n)
        ]
    )
    out_grad, codes = lax.optimization_barrier((out_grad, codes))
    coeff = coefficients(codes)
    w_in16, w_out16 = lax.optimization_barrier(
        (w_in.astype(jnp.bfloat16), w_out.astype(jnp.bfloat16))
    )

    def scaled(shard, owner, earlier=None):
        mine = lax.dynamic_index_in_dim(coeff, (here - owner + n) % n, 0, keepdims=False)
        mine = after(mine, earlier)
        return (mine[:, None] * shard.astype(jnp.float32)).astype(jnp.bfloat16)

    def pre_of(shard):
        return jnp.dot(shard, w_in16, preferred_element_type=jnp.float32)

    def square(pre):
        positive = jnp.maximum(pre, 0.0)
        return (positive * positive).astype(jnp.bfloat16)

    def chain(pre, back):
        return (back * 2.0 * jnp.maximum(pre, 0.0)).astype(jnp.bfloat16)

    token_slots, owners, tokens_came = line_gather(tokens, "col")
    out_grad_slots, _, out_grads_came = line_gather(out_grad, "col")
    parts = next(p for p in (2, 3, 1) if w_out.shape[1] % (128 * p) == 0)
    outs_out = ()

    def update_part(part):
        def run():
            nonlocal outs_out
            outs_out = update(
                acts[-1], dys[-1], grad_out, state_out[part], 256, 16, True, part, parts, outs_out
            )
            return outs_out

        return run

    dys = [scaled(out_grad, here)]
    pre = row_sum(pre_of(tokens), "row")
    acts, dpres = [row_gather(square(pre), "row")], []
    both = jnp.stack([against(dys[0], w_out16), pre_of(token_slots[1])])
    both = row_sum(after(both, (acts[0], tokens_came[1])), "row")
    both, pre = jnp.stack([chain(pre, both[0]), square(both[1])]), both[1]
    last = both = row_gather(both, "row")
    acts.append(both[1])
    dpres.append(both[0])
    for slot in range(1, n):
        if slot > 1:
            last = (last, tokens_came[slot])
            beside, latest = None, None
            if slot == n - 2:
                grad_in = grad_sum(token_slots[:slot], dpres, 256)
                grad_out = grad_sum(acts, dys, 128)
                state_out = fetch((w_out, m_out, v_out), parts)
                beside = [None, (grad_in, grad_out, state_out)]
            if slot == n - 1:
                grad_in = grad_sum(token_slots[slot - 1 : slot], dpres[-1:], 256, (grad_in,))
                grad_out = grad_sum(acts[-1:], dys[-1:], 128, (grad_out,))
                beside, latest = [None, (grad_in, grad_out)], [out_grads_came[slot]]
            pre = row_sum(after(pre_of(token_slots[slot]), last), "row", beside)
            last = row_gather(square(pre), "row", latest)
            acts.append(last)
        if slot < n - 1:
            dys.append(scaled(out_grad_slots[slot], owners[slot]))
            back = after(against(dys[slot], w_out16), (last, out_grads_came[slot]))
            last = row_gather(chain(pre, row_sum(back, "row")), "row")
            dpres.append(last)

    dys.append(scaled(out_grad_slots[n - 1], owners[n - 1], acts[-1]))
    work = [None] + [update_part(part) for part in range(parts)]
    back = row_sum(against(dys[n - 1], w_out16), "row", work)
    dpres.append(row_gather(chain(pre, back), "row", work))
    while work:
        work.pop(0)()
    outs_in = update(token_slots[-1], dpres[-1], grad_in, (w_in, m_in, v_in), 256, 40, False)
    return (*outs_in, *outs_out)


def solution(mesh):
    in_specs = (
        P("col", "row"),
        P("col", "row"),
        P("col"),
        P("col"),
        P("col"),
        P("col"),
        P("row", "col"),
        P("row", "col"),
        P("row", "col"),
        P("col", "row"),
        P("col", "row"),
        P("col", "row"),
    )
    out_specs = (
        P("row", "col"),
        P("row", "col"),
        P("row", "col"),
        P("col", "row"),
        P("col", "row"),
        P("col", "row"),
    )
    return jax.shard_map(
        on_device, mesh=mesh, in_specs=in_specs, out_specs=out_specs, check_vma=False
    )
```

```python
import functools
import math

import jax
import jax.numpy as jnp
from jax import lax
from jax.experimental import pallas as pl
from jax.experimental.pallas import tpu as pltpu
from jax.sharding import PartitionSpec as P

SESSIONS = 8
LIST = 4


def listwise_grad(scores):
    s = scores.reshape(SESSIONS, LIST)
    later = s[:, None, :] - s[:, :, None]
    order = jnp.arange(LIST)
    after = (order[None, :] > order[:, None]).astype(jnp.float32)
    before = (order[None, :] < order[:, None]).astype(jnp.float32)
    worse = -jnp.sum(after[None] * jax.nn.sigmoid(later), axis=2)
    better = jnp.sum(before[None] * jax.nn.sigmoid(-later), axis=2)
    return (worse + better).reshape(SESSIONS * LIST)


def adamw(weight, first, second, grad):
    new_first = 0.9 * first + 0.1 * grad
    new_second = 0.95 * second + 0.05 * (grad * grad)
    scaled = new_second * (1.0 / (1.0 - 0.95**20))
    below = scaled * lax.rsqrt(scaled) + 1e-08
    inverse = pl.reciprocal(below, approx=True)
    inverse = inverse * (2.0 - below * inverse)
    step = (0.0003 / (1.0 - 0.9**20)) * (new_first * inverse)
    return (weight * (1.0 - 0.0003 * 0.1) - step, new_first, new_second)


def over_rows(left, right):
    return lax.dot_general(
        left, right, (((0,), (0,)), ((), ())), preferred_element_type=jnp.float32
    )


def against(left, right):
    return lax.dot_general(
        left, right, (((1,), (1,)), ((), ())), preferred_element_type=jnp.float32
    )


def block_of(size, most):
    block = most
    while size % block:
        block -= 128
    return block


def fetch_kernel(parts, *refs):
    count = (len(refs) - 1) // (parts + 1)
    sources, targets, sems = refs[:count], refs[count:-1], refs[-1]
    copies = []
    for i, target in enumerate(targets):
        part, source = divmod(i, len(sources))
        width = target.shape[1]
        columns = sources[source].at[:, pl.ds(part * width, width)]
        copies.append(pltpu.make_async_copy(columns, target, sems.at[i]))
    for copy in copies:
        copy.start()
    for copy in copies:
        copy.wait()


def fetch(arrays, parts):
    shapes = [pltpu.VMEM((x.shape[0], x.shape[1] // parts), x.dtype) for x in arrays] * parts
    fetched = pl.pallas_call(
        functools.partial(fetch_kernel, parts),
        in_specs=[pl.BlockSpec(memory_space=pltpu.HBM)] * len(arrays),
        out_specs=[pl.BlockSpec(memory_space=pltpu.VMEM)] * len(shapes),
        out_shape=shapes,
        scratch_shapes=[pltpu.SemaphoreType.DMA((len(shapes),))],
        compiler_params=pltpu.CompilerParams(vmem_limit_bytes=4 * 2**20),
        cost_estimate=pl.CostEstimate(
            flops=0, bytes_accessed=4 * sum(x.size for x in arrays), transcendentals=0
        ),
    )(*[pltpu.with_memory_space_constraint(x, pltpu.HBM) for x in arrays])
    return [fetched[i : i + len(arrays)] for i in range(0, len(shapes), len(arrays))]


def grad_kernel(pieces, *refs):
    lefts, rights, out = refs[:pieces], refs[pieces : 2 * pieces], refs[-1]
    total = refs[2 * pieces][...] if len(refs) > 2 * pieces + 1 else 0.0
    for left, right in zip(lefts, rights):
        total += over_rows(left[...], right[...])
    out[...] = total


def grad_sum(lefts, rights, most, so_far=()):
    rows, height = lefts[0].shape
    width = rights[0].shape[1]
    pieces = len(lefts)
    block = block_of(height, most)
    panel = pl.BlockSpec((block, width), lambda i: (i, 0))
    return pl.pallas_call(
        functools.partial(grad_kernel, pieces),
        grid=(height // block,),
        in_specs=[pl.BlockSpec((rows, block), lambda i: (0, i))] * pieces
        + [pl.BlockSpec((rows, width), lambda i: (0, 0))] * pieces
        + [panel] * len(so_far),
        out_specs=panel,
        out_shape=pltpu.VMEM((height, width), jnp.float32),
        input_output_aliases={2 * pieces + i: i for i in range(len(so_far))},
        compiler_params=pltpu.CompilerParams(vmem_limit_bytes=16 * 2**20),
        cost_estimate=pl.CostEstimate(
            flops=2 * pieces * rows * height * width,
            bytes_accessed=4 * height * width + 2 * pieces * rows * (height + width),
            transcendentals=0,
        ),
    )(*lefts, *rights, *so_far)


def update_kernel(left, right, grad, w, m, v, *refs):
    new_w, new_m, new_v = refs[-3:]
    total = grad[...] + over_rows(left[...], right[...])
    new_w[...], new_m[...], new_v[...] = adamw(w[...], m[...], v[...], total)


def update(left, right, grad, w, m, v, most, limit, part=0, parts=1, so_far=()):
    rows, height = left.shape
    width = right.shape[1] // parts
    block = block_of(height, most)
    panel = pl.BlockSpec((block, width), lambda i: (i, part))
    own = pl.BlockSpec((block, width), lambda i: (i, 0))
    shape = jax.ShapeDtypeStruct((height, right.shape[1]), jnp.float32)
    return pl.pallas_call(
        update_kernel,
        grid=(height // block,),
        in_specs=[
            pl.BlockSpec((rows, block), lambda i: (0, i)),
            pl.BlockSpec((rows, width), lambda i: (0, part)),
            panel,
        ]
        + [own] * 3
        + [pl.BlockSpec(memory_space=pl.ANY)] * len(so_far),
        out_specs=[panel] * 3,
        out_shape=[shape] * 3,
        input_output_aliases={6 + i: i for i in range(len(so_far))},
        compiler_params=pltpu.CompilerParams(vmem_limit_bytes=limit * 2**20),
        cost_estimate=pl.CostEstimate(
            flops=2 * rows * height * width,
            bytes_accessed=7 * 4 * height * width + 2 * rows * (height + width),
            transcendentals=2 * height * width,
        ),
    )(left, right, grad, w, m, v, *so_far)


def link_pairs(n, first, step):
    pairs = []
    for low in range(first, n - 1, 2):
        if low - (step - 1) >= 0:
            pairs.append((low, low + 1))
        if low + step <= n - 1:
            pairs.append((low + 1, low))
    return pairs


def arrivals(n, c):
    order = []
    for step in range(1, n):
        from_right, from_left = c + step <= n - 1, c - step >= 0
        over = (from_right, from_left) if c % 2 == 0 else (from_left, from_right)
        order += [(links, step) for links in (0, 1) if over[links]]
    return order


def line_gather(shard, axis):
    n = lax.axis_size(axis)
    here = lax.axis_index(axis)
    came = {(0, 0): shard, (1, 0): shard}
    for step in range(1, n):
        arrived = {}
        for links in (0, 1):
            pairs = link_pairs(n, links, step)
            if pairs:
                arrived[links, step] = lax.ppermute(came[1 - links, step - 1], axis, pairs)
        came.update(lax.optimization_barrier(arrived))
    slots, owners = [shard], [here]
    tables = [arrivals(n, c) for c in range(n)]
    for slot in range(n - 1):
        users = {}
        origins = []
        for c in range(n):
            links, step = tables[c][slot]
            users.setdefault((links, step), []).append(c)
            origins.append(c + step if links == c % 2 else c - step)
        choice = None
        for source, places in users.items():
            if choice is None:
                choice = came[source]
            else:
                mine = functools.reduce(jnp.logical_or, [here == c for c in places])
                choice = jnp.where(mine, came[source], choice)
        slots.append(choice)
        owners.append(jnp.array(origins, dtype=jnp.int32)[here])
    return slots, owners, [[came[at] for at in came if at[1] == step] for step in range(n)]


def after(value, earlier):
    if earlier is not None:
        value, _ = lax.optimization_barrier((value, earlier))
    return value


def exchange(part, axis, mask, beside=None):
    came = lax.ppermute(part, axis, [(i, i ^ mask) for i in range(lax.axis_size(axis))])
    work = beside.pop(0) if beside else None
    return after(came, work() if callable(work) else work)


def row_sum(part, axis, beside=None):
    here = lax.axis_index(axis)
    others = lax.axis_size(axis) // 2
    half = part.shape[-2] // 2
    odd, place = here % 2, here // 2
    kept = lax.dynamic_slice_in_dim(part, odd * half, half, axis=-2)
    sent = lax.dynamic_slice_in_dim(part, (1 - odd) * half, half, axis=-2)
    part = kept + exchange(sent, axis, 1, beside)
    piece = half // others

    def piece_of(which):
        return lax.dynamic_slice_in_dim(part, which * piece, piece, axis=-2)

    came = [exchange(piece_of(place ^ d), axis, 2 * d) for d in range(1, others)]
    work = beside.pop(0) if beside else None
    came = after(came, work() if callable(work) else work)
    return functools.reduce(jnp.add, came, piece_of(place))


def row_gather(part, axis, beside=None, seen=None):
    here = lax.axis_index(axis)
    others = lax.axis_size(axis) // 2
    odd, place = here % 2, here // 2
    pieces = [part] + [exchange(part, axis, 2 * d) for d in range(1, others)]
    work = beside.pop(0) if beside else None
    pieces = after(pieces, work() if callable(work) else work)
    bit = 1
    while bit < others:
        pieces = [
            jnp.where((place // bit) % 2 == 1, pieces[i ^ bit], pieces[i]) for i in range(others)
        ]
        bit *= 2
    part = jnp.concatenate(pieces, axis=-2)
    if seen is not None:
        seen.append(part)
    came = exchange(part, axis, 1, beside)
    return jnp.where(
        odd == 1,
        jnp.concatenate([came, part], axis=-2),
        jnp.concatenate([part, came], axis=-2),
    )


def response_codes(logratio, token_session, token_position, pad_mask):
    live = pad_mask.astype(jnp.float32)
    response = (token_session * LIST + token_position).astype(jnp.float32)
    return jnp.stack([live * logratio, jnp.where(pad_mask != 0, response, -1.0)])


def coefficients(codes):
    n, _, rows = codes.shape
    onehot = (
        codes[:, 1, :, None] == jnp.arange(SESSIONS * LIST, dtype=jnp.float32)
    ).astype(jnp.float32)
    sums = jnp.sum(onehot * codes[:, 0, :, None], axis=(0, 1))
    scores = math.sqrt(SESSIONS * LIST / (n * rows)) * sums
    response_grad = listwise_grad(scores)
    return 0.1 * jnp.sum(onehot * response_grad, axis=2)


def on_device(
    tokens,
    out_grad,
    logratio,
    token_session,
    token_position,
    pad_mask,
    w_in,
    m_in,
    v_in,
    w_out,
    m_out,
    v_out,
):
    n = lax.axis_size("col")
    here = lax.axis_index("col")
    codes = response_codes(logratio, token_session, token_position, pad_mask)
    codes = jnp.stack(
        [codes]
        + [
            lax.ppermute(codes, "col", [(i, (i + shift) % n) for i in range(n)])
            for shift in range(1, n)
        ]
    )
    out_grad, codes = lax.optimization_barrier((out_grad, codes))
    coeff = coefficients(codes)
    w_in16, w_out16 = lax.optimization_barrier(
        (w_in.astype(jnp.bfloat16), w_out.astype(jnp.bfloat16))
    )

    def scaled(shard, owner, earlier=None):
        mine = lax.dynamic_index_in_dim(coeff, (here - owner + n) % n, 0, keepdims=False)
        mine = after(mine, earlier)
        return (mine[:, None] * shard.astype(jnp.float32)).astype(jnp.bfloat16)

    def pre_of(shard):
        return jnp.dot(shard, w_in16, preferred_element_type=jnp.float32)

    def square(pre):
        positive = jnp.maximum(pre, 0.0)
        return (positive * positive).astype(jnp.bfloat16)

    def chain(pre, back):
        return (back * 2.0 * jnp.maximum(pre, 0.0)).astype(jnp.bfloat16)

    token_slots, owners, tokens_came = line_gather(tokens, "col")
    out_grad_slots, _, out_grads_came = line_gather(out_grad, "col")
    parts = next(p for p in (2, 3, 1) if w_out.shape[1] % (128 * p) == 0)
    outs_out = ()

    def update_part(part):
        def run():
            nonlocal outs_out
            outs_out = update(
                acts[-1], dys[-1], grad_out, *state_out[part], 128, 16, part, parts, outs_out
            )
            return outs_out

        return run

    dys = [scaled(out_grad, here)]
    pre = row_sum(pre_of(tokens), "row")
    acts, dpres = [row_gather(square(pre), "row")], []
    both = jnp.stack([against(dys[0], w_out16), pre_of(token_slots[1])])
    both = row_sum(after(both, (acts[0], tokens_came[1])), "row")
    both, pre = jnp.stack([chain(pre, both[0]), square(both[1])]), both[1]
    last = both = row_gather(both, "row")
    acts.append(both[1])
    dpres.append(both[0])
    for slot in range(1, n):
        if slot > 1:
            last = (last, tokens_came[slot])
            beside, latest = None, None
            if slot == n - 2:
                grad_in = grad_sum(token_slots[:slot], dpres, 256)
                grad_out = grad_sum(acts, dys, 128)
                state_out = fetch((w_out, m_out, v_out), parts)
                beside = [None, (grad_in, grad_out, state_out)]
            if slot == n - 1:
                grad_in = grad_sum(token_slots[slot - 1 : slot], dpres[-1:], 256, (grad_in,))
                grad_out = grad_sum(acts[-1:], dys[-1:], 128, (grad_out,))
                beside, latest = [None, (grad_in, grad_out)], [out_grads_came[slot]]
            pre = row_sum(after(pre_of(token_slots[slot]), last), "row", beside)
            last = row_gather(square(pre), "row", latest, seen := [])
            acts.append(last)
        if slot < n - 1:
            dys.append(scaled(out_grad_slots[slot], owners[slot]))
            back = after(against(dys[slot], w_out16), (last, out_grads_came[slot]))
            last = row_gather(chain(pre, row_sum(back, "row")), "row")
            dpres.append(last)

    dys.append(scaled(out_grad_slots[n - 1], owners[n - 1], seen))
    work = [None] + [update_part(part) for part in range(parts)]
    back = row_sum(against(dys[n - 1], w_out16), "row", work)
    dpres.append(row_gather(chain(pre, back), "row", work))
    while work:
        work.pop(0)()
    outs_in = update(token_slots[-1], dpres[-1], grad_in, w_in, m_in, v_in, 256, 42)
    return (*outs_in, *outs_out)


def solution(mesh):
    in_specs = (
        P("col", "row"),
        P("col", "row"),
        P("col"),
        P("col"),
        P("col"),
        P("col"),
        P("row", "col"),
        P("row", "col"),
        P("row", "col"),
        P("col", "row"),
        P("col", "row"),
        P("col", "row"),
    )
    out_specs = (
        P("row", "col"),
        P("row", "col"),
        P("row", "col"),
        P("col", "row"),
        P("col", "row"),
        P("col", "row"),
    )
    return jax.shard_map(
        on_device, mesh=mesh, in_specs=in_specs, out_specs=out_specs, check_vma=False
    )
```

```python
import functools
import math

import jax
import jax.numpy as jnp
from jax import lax
from jax.experimental import pallas as pl
from jax.experimental.pallas import tpu as pltpu
from jax.sharding import PartitionSpec as P

SESSIONS = 8
LIST = 4


def listwise_grad(scores):
    s = scores.reshape(SESSIONS, LIST)
    later = s[:, None, :] - s[:, :, None]
    order = jnp.arange(LIST)
    after = (order[None, :] > order[:, None]).astype(jnp.float32)
    before = (order[None, :] < order[:, None]).astype(jnp.float32)
    worse = -jnp.sum(after[None] * jax.nn.sigmoid(later), axis=2)
    better = jnp.sum(before[None] * jax.nn.sigmoid(-later), axis=2)
    return (worse + better).reshape(SESSIONS * LIST)


def adamw(weight, first, second, grad):
    new_first = 0.9 * first + 0.1 * grad
    new_second = 0.95 * second + 0.05 * (grad * grad)
    scaled = new_second * (1.0 / (1.0 - 0.95**20))
    below = scaled * lax.rsqrt(scaled) + 1e-08
    inverse = pl.reciprocal(below, approx=True)
    inverse = inverse * (2.0 - below * inverse)
    step = (0.0003 / (1.0 - 0.9**20)) * (new_first * inverse)
    return (weight * (1.0 - 0.0003 * 0.1) - step, new_first, new_second)


def over_rows(left, right):
    return lax.dot_general(
        left, right, (((0,), (0,)), ((), ())), preferred_element_type=jnp.float32
    )


def against(left, right):
    return lax.dot_general(
        left, right, (((1,), (1,)), ((), ())), preferred_element_type=jnp.float32
    )


def block_of(size, most):
    block = most
    while size % block:
        block -= 128
    return block


def fetch_kernel(parts, *refs):
    count = (len(refs) - 1) // (parts + 1)
    sources, targets, sems = refs[:count], refs[count:-1], refs[-1]
    copies = []
    for i, target in enumerate(targets):
        part, source = divmod(i, len(sources))
        width = target.shape[1]
        columns = sources[source].at[:, pl.ds(part * width, width)]
        copies.append(pltpu.make_async_copy(columns, target, sems.at[i]))
    for copy in copies:
        copy.start()
    for copy in copies:
        copy.wait()


def fetch(arrays, parts):
    shapes = [pltpu.VMEM((x.shape[0], x.shape[1] // parts), x.dtype) for x in arrays] * parts
    fetched = pl.pallas_call(
        functools.partial(fetch_kernel, parts),
        in_specs=[pl.BlockSpec(memory_space=pltpu.HBM)] * len(arrays),
        out_specs=[pl.BlockSpec(memory_space=pltpu.VMEM)] * len(shapes),
        out_shape=shapes,
        scratch_shapes=[pltpu.SemaphoreType.DMA((len(shapes),))],
        compiler_params=pltpu.CompilerParams(vmem_limit_bytes=4 * 2**20),
        cost_estimate=pl.CostEstimate(
            flops=0, bytes_accessed=4 * sum(x.size for x in arrays), transcendentals=0
        ),
    )(*[pltpu.with_memory_space_constraint(x, pltpu.HBM) for x in arrays])
    return [fetched[i : i + len(arrays)] for i in range(0, len(shapes), len(arrays))]


def grad_kernel(pieces, *refs):
    lefts, rights, out = refs[:pieces], refs[pieces : 2 * pieces], refs[-1]
    total = refs[2 * pieces][...] if len(refs) > 2 * pieces + 1 else 0.0
    for left, right in zip(lefts, rights):
        total += over_rows(left[...], right[...])
    out[...] = total


def grad_sum(lefts, rights, most, so_far=()):
    rows, height = lefts[0].shape
    width = rights[0].shape[1]
    pieces = len(lefts)
    block = block_of(height, most)
    panel = pl.BlockSpec((block, width), lambda i: (i, 0))
    return pl.pallas_call(
        functools.partial(grad_kernel, pieces),
        grid=(height // block,),
        in_specs=[pl.BlockSpec((rows, block), lambda i: (0, i))] * pieces
        + [pl.BlockSpec((rows, width), lambda i: (0, 0))] * pieces
        + [panel] * len(so_far),
        out_specs=panel,
        out_shape=pltpu.VMEM((height, width), jnp.float32),
        input_output_aliases={2 * pieces + i: i for i in range(len(so_far))},
        compiler_params=pltpu.CompilerParams(vmem_limit_bytes=16 * 2**20),
        cost_estimate=pl.CostEstimate(
            flops=2 * pieces * rows * height * width,
            bytes_accessed=4 * height * width + 2 * pieces * rows * (height + width),
            transcendentals=0,
        ),
    )(*lefts, *rights, *so_far)


def update_kernel(left, right, grad, w, m, v, *refs):
    new_w, new_m, new_v = refs[-3:]
    total = grad[...] + over_rows(left[...], right[...])
    new_w[...], new_m[...], new_v[...] = adamw(w[...], m[...], v[...], total)


def update(left, right, grad, w, m, v, most, limit, part=0, parts=1, so_far=()):
    rows, height = left.shape
    width = right.shape[1] // parts
    block = block_of(height, most)
    panel = pl.BlockSpec((block, width), lambda i: (i, part))
    own = pl.BlockSpec((block, width), lambda i: (i, 0))
    shape = jax.ShapeDtypeStruct((height, right.shape[1]), jnp.float32)
    return pl.pallas_call(
        update_kernel,
        grid=(height // block,),
        in_specs=[
            pl.BlockSpec((rows, block), lambda i: (0, i)),
            pl.BlockSpec((rows, width), lambda i: (0, part)),
            panel,
        ]
        + [own] * 3
        + [pl.BlockSpec(memory_space=pl.ANY)] * len(so_far),
        out_specs=[panel] * 3,
        out_shape=[shape] * 3,
        input_output_aliases={6 + i: i for i in range(len(so_far))},
        compiler_params=pltpu.CompilerParams(vmem_limit_bytes=limit * 2**20),
        cost_estimate=pl.CostEstimate(
            flops=2 * rows * height * width,
            bytes_accessed=7 * 4 * height * width + 2 * rows * (height + width),
            transcendentals=2 * height * width,
        ),
    )(left, right, grad, w, m, v, *so_far)


def link_pairs(n, first, step):
    pairs = []
    for low in range(first, n - 1, 2):
        if low - (step - 1) >= 0:
            pairs.append((low, low + 1))
        if low + step <= n - 1:
            pairs.append((low + 1, low))
    return pairs


def arrivals(n, c):
    order = []
    for step in range(1, n):
        from_right, from_left = c + step <= n - 1, c - step >= 0
        over = (from_right, from_left) if c % 2 == 0 else (from_left, from_right)
        order += [(links, step) for links in (0, 1) if over[links]]
    return order


def line_gather(shard, axis):
    n = lax.axis_size(axis)
    here = lax.axis_index(axis)
    came = {(0, 0): shard, (1, 0): shard}
    for step in range(1, n):
        arrived = {}
        for links in (0, 1):
            pairs = link_pairs(n, links, step)
            if pairs:
                arrived[links, step] = lax.ppermute(came[1 - links, step - 1], axis, pairs)
        came.update(lax.optimization_barrier(arrived))
    slots, owners = [shard], [here]
    tables = [arrivals(n, c) for c in range(n)]
    for slot in range(n - 1):
        users = {}
        origins = []
        for c in range(n):
            links, step = tables[c][slot]
            users.setdefault((links, step), []).append(c)
            origins.append(c + step if links == c % 2 else c - step)
        choice = None
        for source, places in users.items():
            if choice is None:
                choice = came[source]
            else:
                mine = functools.reduce(jnp.logical_or, [here == c for c in places])
                choice = jnp.where(mine, came[source], choice)
        slots.append(choice)
        owners.append(jnp.array(origins, dtype=jnp.int32)[here])
    return slots, owners, [[came[at] for at in came if at[1] == step] for step in range(n)]


def after(value, earlier):
    if earlier is not None:
        value, _ = lax.optimization_barrier((value, earlier))
    return value


def exchange(part, axis, mask, beside=None):
    came = lax.ppermute(part, axis, [(i, i ^ mask) for i in range(lax.axis_size(axis))])
    work = beside.pop(0) if beside else None
    return after(came, work() if callable(work) else work)


def row_sum(part, axis, beside=None):
    here = lax.axis_index(axis)
    others = lax.axis_size(axis) // 2
    half = part.shape[-2] // 2
    odd, place = here % 2, here // 2
    kept = lax.dynamic_slice_in_dim(part, odd * half, half, axis=-2)
    sent = lax.dynamic_slice_in_dim(part, (1 - odd) * half, half, axis=-2)
    part = kept + exchange(sent, axis, 1, beside)
    piece = half // others

    def piece_of(which):
        return lax.dynamic_slice_in_dim(part, which * piece, piece, axis=-2)

    came = [exchange(piece_of(place ^ d), axis, 2 * d) for d in range(1, others)]
    work = beside.pop(0) if beside else None
    came = after(came, work() if callable(work) else work)
    return functools.reduce(jnp.add, came, piece_of(place))


def row_gather(part, axis, beside=None, seen=None):
    here = lax.axis_index(axis)
    others = lax.axis_size(axis) // 2
    odd, place = here % 2, here // 2
    pieces = [part] + [exchange(part, axis, 2 * d) for d in range(1, others)]
    work = beside.pop(0) if beside else None
    pieces = after(pieces, work() if callable(work) else work)
    bit = 1
    while bit < others:
        pieces = [
            jnp.where((place // bit) % 2 == 1, pieces[i ^ bit], pieces[i]) for i in range(others)
        ]
        bit *= 2
    part = jnp.concatenate(pieces, axis=-2)
    if seen is not None:
        seen.append(part)
    came = exchange(part, axis, 1, beside)
    return jnp.where(
        odd == 1,
        jnp.concatenate([came, part], axis=-2),
        jnp.concatenate([part, came], axis=-2),
    )


def response_codes(logratio, token_session, token_position, pad_mask):
    live = pad_mask.astype(jnp.float32)
    response = (token_session * LIST + token_position).astype(jnp.float32)
    return jnp.stack([live * logratio, jnp.where(pad_mask != 0, response, -1.0)])


def coefficients(codes):
    n, _, rows = codes.shape
    onehot = (
        codes[:, 1, :, None] == jnp.arange(SESSIONS * LIST, dtype=jnp.float32)
    ).astype(jnp.float32)
    sums = jnp.sum(onehot * codes[:, 0, :, None], axis=(0, 1))
    scores = math.sqrt(SESSIONS * LIST / (n * rows)) * sums
    response_grad = listwise_grad(scores)
    return 0.1 * jnp.sum(onehot * response_grad, axis=2)


def on_device(
    tokens,
    out_grad,
    logratio,
    token_session,
    token_position,
    pad_mask,
    w_in,
    m_in,
    v_in,
    w_out,
    m_out,
    v_out,
):
    n = lax.axis_size("col")
    here = lax.axis_index("col")
    codes = response_codes(logratio, token_session, token_position, pad_mask)
    codes = jnp.stack(
        [codes]
        + [
            lax.ppermute(codes, "col", [(i, (i + shift) % n) for i in range(n)])
            for shift in range(1, n)
        ]
    )
    out_grad, codes = lax.optimization_barrier((out_grad, codes))
    coeff = coefficients(codes)
    w_in16, w_out16 = lax.optimization_barrier(
        (w_in.astype(jnp.bfloat16), w_out.astype(jnp.bfloat16))
    )

    def scaled(shard, owner, earlier=None):
        mine = lax.dynamic_index_in_dim(coeff, (here - owner + n) % n, 0, keepdims=False)
        mine = after(mine, earlier)
        return (mine[:, None] * shard.astype(jnp.float32)).astype(jnp.bfloat16)

    def pre_of(shard):
        return jnp.dot(shard, w_in16, preferred_element_type=jnp.float32)

    def square(pre):
        positive = jnp.maximum(pre, 0.0)
        return (positive * positive).astype(jnp.bfloat16)

    def chain(pre, back):
        return (back * 2.0 * jnp.maximum(pre, 0.0)).astype(jnp.bfloat16)

    token_slots, owners, tokens_came = line_gather(tokens, "col")
    out_grad_slots, _, out_grads_came = line_gather(out_grad, "col")
    parts = next(p for p in (2, 3, 1) if w_out.shape[1] % (128 * p) == 0)
    outs_out = ()

    def update_part(part):
        def run():
            nonlocal outs_out
            outs_out = update(
                acts[-1], dys[-1], grad_out, *state_out[part], 128, 16, part, parts, outs_out
            )
            return outs_out

        return run

    dys = [scaled(out_grad, here)]
    pre = row_sum(pre_of(tokens), "row")
    acts, dpres = [row_gather(square(pre), "row")], []
    both = [against(dys[0], w_out16), pre_of(token_slots[1])]
    both = row_sum(jnp.stack(after(both, (acts[0], tokens_came[1]))), "row")
    both, pre = jnp.stack([chain(pre, both[0]), square(both[1])]), both[1]
    last = both = row_gather(both, "row")
    acts.append(both[1])
    dpres.append(both[0])
    for slot in range(1, n):
        if slot > 1:
            last = (last, tokens_came[slot])
            beside, latest = None, None
            if slot == n - 2:
                grad_in = grad_sum(token_slots[:slot], dpres, 256)
                grad_out = grad_sum(acts, dys, 128)
                state_out = fetch((w_out, m_out, v_out), parts)
                beside = [None, (grad_in, grad_out, state_out)]
            if slot == n - 1:
                grad_in = grad_sum(token_slots[slot - 1 : slot], dpres[-1:], 256, (grad_in,))
                grad_out = grad_sum(acts[-1:], dys[-1:], 128, (grad_out,))
                beside, latest = [None, (grad_in, grad_out)], [out_grads_came[slot]]
            pre = row_sum(after(pre_of(token_slots[slot]), last), "row", beside)
            last = row_gather(square(pre), "row", latest, seen := [])
            acts.append(last)
        if slot < n - 1:
            dys.append(scaled(out_grad_slots[slot], owners[slot]))
            back = after(against(dys[slot], w_out16), (last, out_grads_came[slot]))
            last = row_gather(chain(pre, row_sum(back, "row")), "row")
            dpres.append(last)

    dys.append(scaled(out_grad_slots[n - 1], owners[n - 1], seen))
    work = [None] + [update_part(part) for part in range(parts)]
    back = row_sum(against(dys[n - 1], w_out16), "row", work)
    dpres.append(row_gather(chain(pre, back), "row", work))
    while work:
        work.pop(0)()
    outs_in = update(token_slots[-1], dpres[-1], grad_in, w_in, m_in, v_in, 256, 42)
    return (*outs_in, *outs_out)


def solution(mesh):
    in_specs = (
        P("col", "row"),
        P("col", "row"),
        P("col"),
        P("col"),
        P("col"),
        P("col"),
        P("row", "col"),
        P("row", "col"),
        P("row", "col"),
        P("col", "row"),
        P("col", "row"),
        P("col", "row"),
    )
    out_specs = (
        P("row", "col"),
        P("row", "col"),
        P("row", "col"),
        P("col", "row"),
        P("col", "row"),
        P("col", "row"),
    )
    return jax.shard_map(
        on_device, mesh=mesh, in_specs=in_specs, out_specs=out_specs, check_vma=False
    )
```
